32 devices in a mesh: tile: 4 (over y, x), blk: 8 (over z, core).
Axes of the slice: x: 2, y: 2, z: 4, core: 2. Of those that a mesh axis runs over, the one named last changes fastest.
Arguments:
- tiles: bfloat16 [1536, 8, 8, 2048], P(('blk', 'tile')), may hold values from -10 to 10
- w_reduce: bfloat16 [2048, 512], replicated, may hold values from -0.125 to 0.125
- w_spatial: bfloat16 [9, 512, 512], replicated, may hold values from -0.09375 to 0.09375
- w_expand: bfloat16 [512, 2048], replicated, may hold values from -0.25 to 0.25
- w_embed: bfloat16 [2048, 1536], replicated, may hold values from -0.125 to 0.125
- w_query: bfloat16 [1536, 1536], P(None, 'tile'), may hold values from -8 to 8
- w_key: bfloat16 [1536, 1536], P(None, 'tile'), may hold values from -200 to 200
- w_value: bfloat16 [1536, 1536], P(None, 'tile'), may hold values from -0.15625 to 0.15625
- w_out: bfloat16 [1536, 1536], P('tile'), may hold values from -0.15625 to 0.15625
- slide_tiles: int32 [4], replicated, may hold values from 1 to 1152, 1536 in all
Outputs:
- mixed: bfloat16 [1536, 1536], P(('blk', 'tile'))
The draws below stay inside these ranges and needn't reach their ends.
Inputs may be any that keep to these rules, and one draw needn't show every extreme that they name: `slide_tiles`: the counts sum to 1536 and the largest is exactly 1152.
All inputs are finite; a program needn't handle non-finite values.
Results may differ from the reference program's by a relative error of at most 0.017.
Values may be sent and summed in bfloat16 or wider, within the bound.
No kernel may reach another device: no remote copies, remote signals or barrier semaphores. Data moves between devices by JAX's collectives and lax.ppermute only.
A program may use at most 256 MiB of HBM per device.

```python
import math
import jax
import jax.numpy as jnp
import numpy as np
from jax import lax

C = 2048
MID = 512
SIDE = 8
E = 1536
HEADS = 16
HD = 96
SLIDES = 4
TOKENS = 1536
MOSTLEN = 1152


def draw_tiles(key, part):
    shape = (TOKENS, SIDE, SIDE, C)
    base = jax.random.normal(jax.random.fold_in(key, 1), shape, jnp.float32)
    offset = jax.random.normal(jax.random.fold_in(key, 2), (TOKENS, 1, 1, C), jnp.float32)
    return jnp.clip(base + offset, -10.0, 10.0).astype(jnp.bfloat16)


def query_key_pair(key):
    base = jax.random.normal(jax.random.fold_in(key, 11), (E, E), jnp.float32) / math.sqrt(E)
    other = jax.random.normal(jax.random.fold_in(key, 12), (E, E), jnp.float32) / math.sqrt(E)
    key_weight = other
    return (jnp.clip(base, -8.0, 8.0), jnp.clip(key_weight, -200.0, 200.0))


def draw_w_query(key, part):
    return query_key_pair(key)[0].astype(jnp.bfloat16)


def draw_w_key(key, part):
    return query_key_pair(key)[1].astype(jnp.bfloat16)


def block_levels(own_key, dims, shards, low, top_value):
    def one(axis_at, shards_of):
        heights = jax.random.uniform(jax.random.fold_in(jax.random.fold_in(own_key, 6), axis_at), (shards_of,), jnp.float32, low / len(shards), top_value / len(shards))
        return jnp.repeat(jnp.exp(heights), dims[axis_at] // shards_of).reshape((-1,) + (1,) * (len(dims) - axis_at - 1))

    factor_of = one(*shards[0])
    for cut in shards[1:]:
        factor_of = factor_of * one(*cut)
    return factor_of


def profile(number_of, total, bound, lean):
    portions = [(1 << 20) // math.isqrt(standing ** lean) + 1 for standing in range(2, number_of + 1)]
    rest, holding = total - bound - (number_of - 1), [1] * (number_of - 1)
    while rest > 0:
        candidates = [i for i in range(number_of - 1) if holding[i] < bound]
        mass, remaining = sum([portions[i] for i in candidates]), rest
        for i in candidates:
            extra = min(bound - holding[i], max(1, remaining * portions[i] // mass), rest)
            holding[i] = holding[i] + extra
            rest = rest - extra
    return np.array([bound] + holding)


def ragged_sizes(own_key, number_of, total, limit, lean):
    if number_of == 2:
        one = jax.random.randint(own_key, (), max(1, total - limit), min(limit, total - 1) + 1)
        return jnp.stack([one, total - one])
    sizes = jnp.asarray(profile(number_of, total, limit, lean), jnp.int32)
    twos = (number_of - 1) // 2
    source_of, sink = sizes[1:1 + 2 * twos:2], sizes[2:2 + 2 * twos:2]
    room = jnp.minimum(source_of - 1, limit - sink)
    passed = jax.random.randint(jax.random.fold_in(own_key, 1), (twos,), 0, 1 << 20) % (room + 1)
    sizes = sizes.at[1:1 + 2 * twos:2].set(source_of - passed).at[2:2 + 2 * twos:2].set(sink + passed)
    return sizes[jax.random.permutation(jax.random.fold_in(own_key, 2), number_of)]


def scatter_about(stream_key, dims, scale, reach, pieces=(), kind=jnp.bfloat16):
    array = scale * jax.random.normal(stream_key, dims, jnp.float32)
    if pieces:
        array = array * block_levels(stream_key, dims, pieces, -0.22, 0.18)
    return jnp.clip(array, -reach, reach).astype(kind)


def setup_inputs(seed: int = 0) -> dict:
    splits = jax.random.split(jax.random.key(seed), 11)
    return {
        "tiles": draw_tiles(jax.random.fold_in(splits[10], 71), 0),
        "w_reduce": scatter_about(splits[1], (C, MID), C ** -0.5, 0.125),
        "w_spatial": scatter_about(splits[2], (9, MID, MID), (9 * MID) ** -0.5, 0.09375),
        "w_expand": scatter_about(splits[3], (MID, C), MID ** -0.5, 0.25),
        "w_embed": scatter_about(splits[4], (C, E), C ** -0.5, 0.125),
        "w_query": draw_w_query(jax.random.fold_in(splits[10], 71), 0),
        "w_key": draw_w_key(jax.random.fold_in(splits[10], 71), 0),
        "w_value": scatter_about(splits[7], (E, E), E ** -0.5, 0.15625, ((1, 4),)),
        "w_out": scatter_about(splits[8], (E, E), E ** -0.5, 0.15625, ((0, 4),)),
        "slide_tiles": ragged_sizes(splits[9], SLIDES, TOKENS, MOSTLEN, 2).astype(jnp.int32),
    }


def encode(block, w_reduce, w_spatial, w_expand, w_embed):
    count = block.shape[0]
    flat = block.reshape(count * SIDE * SIDE, C)
    reduced = jax.nn.relu(jnp.dot(flat, w_reduce, preferred_element_type=jnp.float32)).astype(jnp.bfloat16)
    reduced = reduced.reshape(count, SIDE, SIDE, MID)
    padded = jnp.pad(reduced, ((0, 0), (1, 1), (1, 1), (0, 0)))
    summed = jnp.zeros((count * SIDE * SIDE, MID), jnp.float32)
    for tap in range(9):
        row_off = tap // 3
        col_off = tap % 3
        window = padded[:, row_off:row_off + SIDE, col_off:col_off + SIDE, :].reshape(count * SIDE * SIDE, MID)
        summed = summed + jnp.dot(window, w_spatial[tap], preferred_element_type=jnp.float32)
    spatial = jax.nn.relu(summed).astype(jnp.bfloat16)
    output = jax.nn.relu(flat.astype(jnp.float32) + jnp.dot(spatial, w_expand, preferred_element_type=jnp.float32))
    pooled = (lax.optimization_barrier(jnp.sum(output.reshape(count, SIDE * SIDE, C), axis=1)) / (SIDE * SIDE)).astype(jnp.bfloat16)
    return jnp.dot(pooled, w_embed, preferred_element_type=jnp.float32).astype(jnp.bfloat16)

def normalize(rows):
    values = rows.astype(jnp.float32)
    center = lax.optimization_barrier(jnp.mean(values, axis=1, keepdims=True))
    spread = lax.optimization_barrier(jnp.mean((values - center) ** 2, axis=1, keepdims=True))
    return ((values - center) * lax.rsqrt(spread + 1e-05)).astype(jnp.bfloat16)

def slide_of(positions, slide_tiles):
    ends = jnp.cumsum(slide_tiles)[:-1].astype(jnp.int32)
    return lax.optimization_barrier(jnp.sum((positions[:, None] >= ends[None, :]).astype(jnp.int32), axis=1))

def reference(tiles, w_reduce, w_spatial, w_expand, w_embed, w_query, w_key, w_value, w_out, slide_tiles):
    blocks = tiles.reshape(TOKENS // 16, 16, SIDE, SIDE, C)
    emb = lax.map(lambda block: encode(block, w_reduce, w_spatial, w_expand, w_embed), blocks).reshape(TOKENS, E)
    normed = normalize(emb)
    query = jnp.dot(normed, w_query, preferred_element_type=jnp.float32).astype(jnp.bfloat16)
    key = jnp.dot(normed, w_key, preferred_element_type=jnp.float32).astype(jnp.bfloat16)
    value = jnp.dot(normed, w_value, preferred_element_type=jnp.float32).astype(jnp.bfloat16)
    slide = slide_of(jnp.arange(TOKENS, dtype=jnp.int32), slide_tiles)
    same = slide[:, None] == slide[None, :]
    scale = 1.0 / math.sqrt(HD)

    def per_head(operands):
        head_query, head_key, head_value = operands
        scores = jnp.dot(head_query, head_key.T, preferred_element_type=jnp.float32) * scale
        scores = jnp.where(same, scores, -1e+30)
        top = lax.optimization_barrier(jnp.max(scores, axis=1, keepdims=True))
        probs = jnp.where(same, jnp.exp(scores - top), 0.0)
        total = lax.optimization_barrier(jnp.sum(probs, axis=1, keepdims=True))
        return jnp.dot(probs.astype(jnp.bfloat16), head_value, preferred_element_type=jnp.float32) / total
    split_query = query.reshape(TOKENS, HEADS, HD).transpose(1, 0, 2)
    split_key = key.reshape(TOKENS, HEADS, HD).transpose(1, 0, 2)
    split_value = value.reshape(TOKENS, HEADS, HD).transpose(1, 0, 2)
    heads_out = lax.map(per_head, (split_query, split_key, split_value))
    attended = heads_out.transpose(1, 0, 2).reshape(TOKENS, E).astype(jnp.bfloat16)
    mixed = emb.astype(jnp.float32) + jnp.dot(attended, w_out, preferred_element_type=jnp.float32)
    return mixed.astype(jnp.bfloat16)
```

```python
import functools
import math

import jax
import jax.numpy as jnp
from jax import lax
from jax.experimental import pallas as pl
from jax.experimental.pallas import tpu as pltpu
from jax.sharding import PartitionSpec as P

SIDE = 8
HD = 96
LANES = 128
F32 = jnp.float32
BF16 = jnp.bfloat16
GROUP = 8


def dot(a, b):
    return jnp.dot(a, b, preferred_element_type=F32)


def neighbours(rows):
    col = lax.broadcasted_iota(jnp.int32, rows.shape, 1)
    left = jnp.where(col >= 1, pltpu.roll(rows, 1, axis=1), 0.0)
    right = jnp.where(col <= SIDE - 2, pltpu.roll(rows, SIDE - 1, axis=1), 0.0)
    return left, rows, right


def bottleneck(x, wr, ws, we, waits):
    total = x.shape[0]
    count = total // (SIDE * SIDE)
    mid = wr.shape[1]
    band = count * SIDE
    waits[0]()
    reduced = jnp.maximum(dot(x, wr[...]), 0.0)
    reduced = reduced.reshape(count, SIDE, SIDE, mid).swapaxes(0, 1).reshape(band, SIDE, mid)
    taps = jnp.concatenate([p.reshape(total, mid).astype(BF16) for p in neighbours(reduced)], axis=1)
    waits[1]()
    edge = jnp.zeros((band, mid), F32)
    summed = dot(taps, ws[1])
    summed = summed + jnp.concatenate([edge, dot(taps[:-band], ws[0])], axis=0)
    summed = summed + jnp.concatenate([dot(taps[band:], ws[2]), edge], axis=0)
    spatial = jnp.maximum(summed, 0.0).reshape(SIDE, count, SIDE, mid).swapaxes(0, 1)
    spatial = spatial.reshape(total, mid).astype(BF16)
    waits[2]()
    out = jnp.maximum(dot(spatial, we[...]) + x.astype(F32), 0.0)
    return jnp.sum(out.reshape(count, SIDE * SIDE, x.shape[1]), axis=1) * (1.0 / (SIDE * SIDE))


def encode_kernel(x, wr_hbm, ws_hbm, we_hbm, wm_hbm, emb, wr, ws, we, wm, pooled, sems):
    step = pl.program_id(0)
    last = pl.num_programs(0) - 1
    copies = [
        pltpu.make_async_copy(src, dst, sems.at[i])
        for i, (src, dst) in enumerate(((wr_hbm, wr), (ws_hbm, ws), (we_hbm, we), (wm_hbm, wm)))
    ]

    def run(waits):
        count = x.shape[0] // (SIDE * SIDE)
        value = bottleneck(x[...], wr, ws, we, waits)
        pooled[pl.ds(pl.multiple_of(step * count, count), count), :] = value

    @pl.when(step == 0)
    def _():
        for copy in copies:
            copy.start()
        run([copy.wait for copy in copies])

    @pl.when(step > 0)
    def _():
        run([lambda: None] * 3)

    @pl.when(step == last)
    def _():
        copies[3].wait()
        emb[...] = dot(pooled[...].astype(BF16), wm[...]).astype(BF16)


def encode(flat, wr, ws, we, wm):
    total, c = flat.shape
    count = total // (SIDE * SIDE)
    rows = GROUP * SIDE * SIDE
    anywhere = pl.BlockSpec(memory_space=pl.ANY)
    return pl.pallas_call(
        encode_kernel,
        grid=(count // GROUP,),
        in_specs=[pl.BlockSpec((rows, c), lambda i: (i, 0))] + [anywhere] * 4,
        out_specs=pl.BlockSpec((count, wm.shape[1]), lambda i: (0, 0)),
        out_shape=jax.ShapeDtypeStruct((count, wm.shape[1]), BF16),
        scratch_shapes=[
            pltpu.VMEM(wr.shape, BF16),
            pltpu.VMEM(ws.shape, BF16),
            pltpu.VMEM(we.shape, BF16),
            pltpu.VMEM(wm.shape, BF16),
            pltpu.VMEM((count, c), F32),
            pltpu.SemaphoreType.DMA((4,)),
        ],
        compiler_params=pltpu.CompilerParams(vmem_limit_bytes=56 << 20),
        name="encode",
    )(flat, wr, ws, we, wm)


def project_kernel(heads, spread_of, emb, wq, wk, wv, *outs):
    a = lax.axis_index("blk") // spread_of
    scratch = outs[-1]
    values = emb[...].astype(F32)
    center = jnp.mean(values, axis=1, keepdims=True)
    values = values - center
    spread = jnp.mean(values * values, axis=1, keepdims=True)
    normed = (values * lax.rsqrt(spread + 1e-05)).astype(BF16)
    scratch[...] = jnp.zeros_like(scratch)
    for part, w in enumerate((wq, wk, wv)):
        result = dot(normed, w[...]).astype(BF16)
        for head in range(heads):
            scratch[head, :, part * LANES : part * LANES + HD] = result[:, head * HD : (head + 1) * HD]
    for e in range(heads):
        outs[e][...] = scratch[a ^ e]


def project(emb, wq, wk, wv, heads, spread_of):
    rows = emb.shape[0]
    return pl.pallas_call(
        functools.partial(project_kernel, heads, spread_of),
        out_shape=[jax.ShapeDtypeStruct((rows, 3 * LANES), BF16)] * heads,
        scratch_shapes=[pltpu.VMEM((heads, rows, 3 * LANES), BF16)],
        compiler_params=pltpu.CompilerParams(vmem_limit_bytes=24 << 20),
        name="project",
    )(emb, wq, wk, wv)


def attend_kernel(heads, spread_of, tiles_of, slide_tiles, *refs):
    own = refs[:heads]
    others = refs[heads : heads + spread_of - 1]
    out, keys, values = refs[heads + spread_of - 1 :]
    blk = lax.axis_index("blk")
    a, c = blk // spread_of, lax.rem(blk, spread_of)
    length = own[0].shape[0]
    count = length // tiles_of
    ends = [slide_tiles[0], slide_tiles[0] + slide_tiles[1]]
    ends.append(ends[1] + slide_tiles[2])

    def slide_of(shape, dim, start):
        pos = lax.broadcasted_iota(jnp.int32, shape, dim) + start
        return sum((pos >= end).astype(jnp.int32) for end in ends)

    slides = []
    lane = lax.broadcasted_iota(jnp.int32, (length, LANES), 1)
    for f in range(spread_of):
        for e in range(heads):
            at = (f * heads + e) * length
            if f == 0:
                keys[at : at + length] = own[e][:, LANES : 2 * LANES]
                value = own[e][:, 2 * LANES :]
            else:
                keys[at : at + length] = others[f - 1][e * length : (e + 1) * length, :LANES]
                value = others[f - 1][e * length : (e + 1) * length, LANES:]
            values[at : at + length] = jnp.where(lane == HD, 1.0, value.astype(F32)).astype(BF16)
            slides.append(slide_of((1, length), 1, ((a ^ e) * spread_of + (c ^ f)) * length))
    key_slide = jnp.concatenate(slides, axis=1)
    scale = math.log2(math.e) / math.sqrt(HD)
    me = lax.axis_index("tile")
    for e in range(heads):
        query = own[e][:, :LANES]
        query_slide = slide_of((length, 1), 0, ((a ^ e) * spread_of + c) * length)
        scores = lax.dot_general(
            query, keys[...], (((1,), (1,)), ((), ())), preferred_element_type=F32
        )
        scores = jnp.where(query_slide == key_slide, scores, -1e30)
        top = jnp.max(scores, axis=1, keepdims=True)
        weights = jnp.exp2((scores - top) * scale).astype(BF16)
        product = dot(weights, values[...])
        result = (product / product[:, HD : HD + 1]).astype(BF16)
        for t in range(tiles_of):
            out[t * heads + (a ^ e)] = result[t * count : (t + 1) * count]


def attend(slide_tiles, own, others, heads, spread_of, tiles_of):
    length = own[0].shape[0]
    total = length * heads * spread_of
    whole = pl.BlockSpec(memory_space=pltpu.VMEM)
    return pl.pallas_call(
        functools.partial(attend_kernel, heads, spread_of, tiles_of),
        in_specs=[pl.BlockSpec(memory_space=pltpu.SMEM)] + [whole] * (heads + spread_of - 1),
        out_specs=whole,
        out_shape=jax.ShapeDtypeStruct((tiles_of * heads, length // tiles_of, LANES), BF16),
        scratch_shapes=[pltpu.VMEM((total, LANES), BF16), pltpu.VMEM((total, LANES), BF16)],
        compiler_params=pltpu.CompilerParams(vmem_limit_bytes=40 << 20),
        name="attend",
    )(slide_tiles, *own, *others)


def finish_kernel(parts, w_out, emb, out):
    attended = jnp.concatenate([parts[h][:, :HD].astype(F32) for h in range(parts.shape[0])], axis=1)
    out[...] = (emb[...].astype(F32) + dot(attended.astype(BF16), w_out[...])).astype(BF16)


def finish(parts, w_out, emb):
    return pl.pallas_call(
        finish_kernel,
        out_shape=jax.ShapeDtypeStruct(emb.shape, BF16),
        compiler_params=pltpu.CompilerParams(vmem_limit_bytes=24 << 20),
        name="finish",
    )(parts, w_out, emb)


def shards(tiles_of, blks, tiles, wr, ws, we, wm, wq, wk, wv, wo, slide_tiles):
    count = tiles.shape[0]
    flat = tiles.reshape(count * SIDE * SIDE, tiles.shape[3])
    mid = wr.shape[1]
    heads = wq.shape[1] // HD
    spread_of = blks // heads
    w_out = lax.all_gather(wo, "tile", axis=0, tiled=True)
    emb = encode(flat, wr, ws.reshape(3, 3 * mid, mid), we, wm)
    gathered = lax.all_gather(emb, "tile", axis=0, tiled=True)
    mine = project(gathered, wq, wk, wv, heads, spread_of)
    own = [mine[0]]
    for e in range(1, heads):
        pairs = [(i, i ^ (e * spread_of)) for i in range(blks)]
        own.append(lax.ppermute(mine[e], "blk", pairs))
    key_value = jnp.concatenate([piece[:, LANES:] for piece in own], axis=0)
    others = [
        lax.ppermute(key_value, "blk", [(i, i ^ f) for i in range(blks)]) for f in range(1, spread_of)
    ]
    attended = attend(slide_tiles, own, others, heads, spread_of, tiles_of)
    groups = [
        [t * blks + a * spread_of + c for t in range(tiles_of) for a in range(heads)]
        for c in range(spread_of)
    ]
    parts = lax.all_to_all(attended, ("tile", "blk"), 0, 0, axis_index_groups=groups, tiled=True)
    return finish(parts, w_out, emb)


def solution(mesh):
    placed = (
        P(("blk", "tile"), None, None, None),
        P(),
        P(),
        P(),
        P(),
        P(None, "tile"),
        P(None, "tile"),
        P(None, "tile"),
        P("tile", None),
        P(),
    )
    return jax.shard_map(
        functools.partial(shards, mesh.shape["tile"], mesh.shape["blk"]),
        mesh=mesh,
        in_specs=placed,
        out_specs=P(("blk", "tile"), None),
        check_vma=False,
    )
```

```python
import functools
import math

import jax
import jax.numpy as jnp
from jax import lax
from jax.experimental import pallas as pl
from jax.experimental.pallas import tpu as pltpu
from jax.sharding import PartitionSpec as P

SIDE = 8
HD = 96
THIRD = HD // 3
LANES = 128
F32 = jnp.float32
BF16 = jnp.bfloat16
GROUP = 8


def dot(a, b):
    return jnp.dot(a, b, preferred_element_type=F32)


def neighbours(rows):
    col = lax.broadcasted_iota(jnp.int32, rows.shape, 1)
    left = jnp.where(col >= 1, pltpu.roll(rows, 1, axis=1), 0.0)
    right = jnp.where(col <= SIDE - 2, pltpu.roll(rows, SIDE - 1, axis=1), 0.0)
    return left, rows, right


def bottleneck(x, wr, ws, we, waits):
    total = x.shape[0]
    count = total // (SIDE * SIDE)
    mid = wr.shape[1]
    band = count * SIDE
    waits[0]()
    reduced = jnp.maximum(dot(x, wr[...]), 0.0)
    reduced = reduced.reshape(count, SIDE, SIDE, mid).swapaxes(0, 1).reshape(band, SIDE, mid)
    taps = jnp.concatenate([p.reshape(total, mid).astype(BF16) for p in neighbours(reduced)], axis=1)
    waits[1]()
    edge = jnp.zeros((band, mid), F32)
    summed = dot(taps, ws[1])
    summed = summed + jnp.concatenate([edge, dot(taps[:-band], ws[0])], axis=0)
    summed = summed + jnp.concatenate([dot(taps[band:], ws[2]), edge], axis=0)
    spatial = jnp.maximum(summed, 0.0).reshape(SIDE, count, SIDE, mid).swapaxes(0, 1)
    spatial = spatial.reshape(total, mid).astype(BF16)
    waits[2]()
    out = jnp.maximum(dot(spatial, we[...]) + x.astype(F32), 0.0)
    return jnp.sum(out.reshape(count, SIDE * SIDE, x.shape[1]), axis=1) * (1.0 / (SIDE * SIDE))


def encode_kernel(x, wr_hbm, ws_hbm, we_hbm, wm_hbm, emb, wr, ws, we, wm, pooled, sems):
    step = pl.program_id(0)
    last = pl.num_programs(0) - 1
    copies = [
        pltpu.make_async_copy(src, dst, sems.at[i])
        for i, (src, dst) in enumerate(((wr_hbm, wr), (ws_hbm, ws), (we_hbm, we), (wm_hbm, wm)))
    ]

    def run(waits):
        count = x.shape[0] // (SIDE * SIDE)
        value = bottleneck(x[...], wr, ws, we, waits)
        pooled[pl.ds(pl.multiple_of(step * count, count), count), :] = value

    @pl.when(step == 0)
    def _():
        for copy in copies:
            copy.start()
        run([copy.wait for copy in copies])

    @pl.when(step > 0)
    def _():
        run([lambda: None] * 3)

    @pl.when(step == last)
    def _():
        copies[3].wait()
        emb[...] = dot(pooled[...].astype(BF16), wm[...]).astype(BF16)


def encode(flat, wr, ws, we, wm):
    total, c = flat.shape
    count = total // (SIDE * SIDE)
    rows = GROUP * SIDE * SIDE
    anywhere = pl.BlockSpec(memory_space=pl.ANY)
    return pl.pallas_call(
        encode_kernel,
        grid=(count // GROUP,),
        in_specs=[pl.BlockSpec((rows, c), lambda i: (i, 0))] + [anywhere] * 4,
        out_specs=pl.BlockSpec((count, wm.shape[1]), lambda i: (0, 0)),
        out_shape=jax.ShapeDtypeStruct((count, wm.shape[1]), BF16),
        scratch_shapes=[
            pltpu.VMEM(wr.shape, BF16),
            pltpu.VMEM(ws.shape, BF16),
            pltpu.VMEM(we.shape, BF16),
            pltpu.VMEM(wm.shape, BF16),
            pltpu.VMEM((count, c), F32),
            pltpu.SemaphoreType.DMA((4,)),
        ],
        compiler_params=pltpu.CompilerParams(vmem_limit_bytes=56 << 20),
        name="encode",
    )(flat, wr, ws, we, wm)


def project_kernel(heads, spread_of, emb, wq, wk, wv, *outs):
    a = lax.axis_index("blk") // spread_of
    scratch = outs[-1]
    rows = emb.shape[0]
    values = emb[...].astype(F32)
    center = jnp.mean(values, axis=1, keepdims=True)
    values = values - center
    spread = jnp.mean(values * values, axis=1, keepdims=True)
    normed = (values * lax.rsqrt(spread + 1e-05)).astype(BF16)
    query, key, value = (dot(normed, w[...]) for w in (wq, wk, wv))
    for head in range(heads):
        q, k, v = (r[:, head * HD : (head + 1) * HD] for r in (query, key, value))
        first = jnp.concatenate([q, v[:, 2 * THIRD :]], axis=1)
        second = jnp.concatenate([k, v[:, THIRD : 2 * THIRD]], axis=1)
        quarter = rows // 4
        third = jnp.concatenate([v[i * quarter : (i + 1) * quarter, :THIRD] for i in range(4)], axis=1)
        scratch[head] = jnp.concatenate([first, second, third], axis=0).astype(BF16)
    for e in range(heads):
        outs[e][...] = scratch[a ^ e]


def project(emb, wq, wk, wv, heads, spread_of):
    rows = emb.shape[0]
    packed = 2 * rows + rows // 4
    return pl.pallas_call(
        functools.partial(project_kernel, heads, spread_of),
        out_shape=[jax.ShapeDtypeStruct((packed, LANES), BF16)] * heads,
        scratch_shapes=[pltpu.VMEM((heads, packed, LANES), BF16)],
        compiler_params=pltpu.CompilerParams(vmem_limit_bytes=24 << 20),
        name="project",
    )(emb, wq, wk, wv)


def unpack_kernel(heads, *refs):
    own, out = refs[:heads], refs[heads]
    rows = own[0].shape[0] * 4 // 9
    quarter = rows // 4
    lane = lax.broadcasted_iota(jnp.int32, (rows, LANES), 1)
    for e in range(heads):
        first = own[e][:rows].astype(F32)
        second = own[e][rows : 2 * rows].astype(F32)
        third = own[e][2 * rows :].astype(F32)
        low = jnp.concatenate(
            [third] + [pltpu.roll(third, LANES - i * THIRD, axis=1) for i in range(1, 4)], axis=0
        )
        middle = pltpu.roll(second, 2 * THIRD, axis=1)
        high = pltpu.roll(first, 3 * THIRD, axis=1)
        value = jnp.where(lane < THIRD, low, jnp.where(lane < 2 * THIRD, middle, high))
        value = jnp.where(lane < HD, value, jnp.where(lane == HD, 1.0, 0.0))
        key = jnp.where(lane < HD, second, 0.0)
        out[e * rows : (e + 1) * rows, :LANES] = key.astype(BF16)
        out[e * rows : (e + 1) * rows, LANES:] = value.astype(BF16)


def unpack(own):
    rows = own[0].shape[0] * 4 // 9
    return pl.pallas_call(
        functools.partial(unpack_kernel, len(own)),
        out_shape=jax.ShapeDtypeStruct((len(own) * rows, 2 * LANES), BF16),
        compiler_params=pltpu.CompilerParams(vmem_limit_bytes=24 << 20),
        name="unpack",
    )(*own)


def attend_kernel(heads, spread_of, tiles_of, slide_tiles, *refs):
    own = refs[:heads]
    sets = refs[heads : heads + spread_of]
    out = refs[heads + spread_of]
    blk = lax.axis_index("blk")
    a, c = blk // spread_of, lax.rem(blk, spread_of)
    length = sets[0].shape[0] // heads
    count = length // tiles_of
    ends = [slide_tiles[0], slide_tiles[0] + slide_tiles[1]]
    ends.append(ends[1] + slide_tiles[2])

    def slide_of(shape, dim, start):
        pos = lax.broadcasted_iota(jnp.int32, shape, dim) + start
        return sum((pos >= end).astype(jnp.int32) for end in ends)

    key_slides = [
        jnp.concatenate(
            [slide_of((1, length), 1, ((a ^ e) * spread_of + (c ^ f)) * length) for e in range(heads)],
            axis=1,
        )
        for f in range(spread_of)
    ]
    scale = math.log2(math.e) / math.sqrt(HD)
    for e in range(heads):
        query = own[e][:length]
        query_slide = slide_of((length, 1), 0, ((a ^ e) * spread_of + c) * length)
        scores = []
        for f in range(spread_of):
            part = lax.dot_general(
                query, sets[f][:, :LANES], (((1,), (1,)), ((), ())), preferred_element_type=F32
            )
            scores.append(jnp.where(query_slide == key_slides[f], part, -1e30))
        top = functools.reduce(jnp.maximum, [jnp.max(s, axis=1, keepdims=True) for s in scores])
        product = sum(
            dot(jnp.exp2((s - top) * scale).astype(BF16), sets[f][:, LANES:])
            for f, s in enumerate(scores)
        )
        result = (product / product[:, HD : HD + 1]).astype(BF16)
        for t in range(tiles_of):
            out[t * heads + (a ^ e)] = result[t * count : (t + 1) * count]


def attend(slide_tiles, own, sets, tiles_of):
    heads, spread_of = len(own), len(sets)
    length = sets[0].shape[0] // heads
    whole = pl.BlockSpec(memory_space=pltpu.VMEM)
    return pl.pallas_call(
        functools.partial(attend_kernel, heads, spread_of, tiles_of),
        in_specs=[pl.BlockSpec(memory_space=pltpu.SMEM)] + [whole] * (heads + spread_of),
        out_specs=whole,
        out_shape=jax.ShapeDtypeStruct((tiles_of * heads, length // tiles_of, LANES), BF16),
        compiler_params=pltpu.CompilerParams(vmem_limit_bytes=40 << 20),
        name="attend",
    )(slide_tiles, *own, *sets)


def finish_kernel(heads, order, parts, emb, *refs):
    out = refs[-1]
    total = emb[...].astype(F32)
    for where, w in zip(order(), refs[:-1]):
        attended = jnp.concatenate(
            [parts[where * heads + h][:, :HD].astype(F32) for h in range(w.shape[0] // HD)], axis=1
        )
        total = total + dot(attended.astype(BF16), w[...])
    out[...] = total.astype(BF16)


def finish(parts, emb, w_outs, heads, order):
    return pl.pallas_call(
        functools.partial(finish_kernel, heads, order),
        out_shape=jax.ShapeDtypeStruct(emb.shape, BF16),
        compiler_params=pltpu.CompilerParams(vmem_limit_bytes=24 << 20),
        name="finish",
    )(parts, emb, *w_outs)


def gather_w_out(w_out, tiles_of, blks):
    if tiles_of != 4:
        return [lax.all_gather(w_out, "tile", axis=0, tiled=True)], lambda: (0,)

    def fetch(x, flip):
        pairs = [
            (t * blks + b, (t ^ flip[b % 2]) * blks + b) for t in range(tiles_of) for b in range(blks)
        ]
        return lax.ppermute(x, ("tile", "blk"), pairs)

    first = fetch(w_out, (1, 2))
    second = lax.ppermute(first, "blk", [(b, b ^ 1) for b in range(blks)])
    third = fetch(first, (2, 1))

    def order():
        t, core = lax.axis_index("tile"), lax.rem(lax.axis_index("blk"), 2)
        return t, t ^ (1 + core), t ^ (2 - core), t ^ 3

    return [w_out, first, second, third], order


def shards(tiles_of, blks, tiles, wr, ws, we, wm, wq, wk, wv, wo, slide_tiles):
    count = tiles.shape[0]
    flat = tiles.reshape(count * SIDE * SIDE, tiles.shape[3])
    mid = wr.shape[1]
    heads = wq.shape[1] // HD
    spread_of = blks // heads
    w_outs, order = gather_w_out(wo, tiles_of, blks)
    emb = encode(flat, wr, ws.reshape(3, 3 * mid, mid), we, wm)
    gathered = lax.all_gather(emb, "tile", axis=0, tiled=True)
    mine = project(gathered, wq, wk, wv, heads, spread_of)
    own = [mine[0]]
    for e in range(1, heads):
        pairs = [(i, i ^ (e * spread_of)) for i in range(blks)]
        own.append(lax.ppermute(mine[e], "blk", pairs))
    sets = [unpack(own)]
    for f in range(1, spread_of):
        sets.append(lax.ppermute(sets[0], "blk", [(i, i ^ f) for i in range(blks)]))
    attended = attend(slide_tiles, own, sets, tiles_of)
    groups = [
        [t * blks + a * spread_of + c for t in range(tiles_of) for a in range(heads)]
        for c in range(spread_of)
    ]
    parts = lax.all_to_all(attended, ("tile", "blk"), 0, 0, axis_index_groups=groups, tiled=True)
    return finish(parts, emb, w_outs, heads, order)


def solution(mesh):
    placed = (
        P(("blk", "tile"), None, None, None),
        P(),
        P(),
        P(),
        P(),
        P(None, "tile"),
        P(None, "tile"),
        P(None, "tile"),
        P("tile", None),
        P(),
    )
    return jax.shard_map(
        functools.partial(shards, mesh.shape["tile"], mesh.shape["blk"]),
        mesh=mesh,
        in_specs=placed,
        out_specs=P(("blk", "tile"), None),
        check_vma=False,
    )
```

```python
import functools
import math

import jax
import jax.numpy as jnp
from jax import lax
from jax.experimental import pallas as pl
from jax.experimental.pallas import tpu as pltpu
from jax.sharding import PartitionSpec as P

SIDE = 8
HD = 96
THIRD = HD // 3
LANES = 128
F32 = jnp.float32
BF16 = jnp.bfloat16
GROUP = 8


def dot(a, b):
    return jnp.dot(a, b, preferred_element_type=F32)


def neighbours(rows):
    col = lax.broadcasted_iota(jnp.int32, rows.shape, 1)
    left = jnp.where(col >= 1, pltpu.roll(rows, 1, axis=1), 0.0)
    right = jnp.where(col <= SIDE - 2, pltpu.roll(rows, SIDE - 1, axis=1), 0.0)
    return left, rows, right


def bottleneck(x, wr, ws, we, waits):
    total = x.shape[0]
    count = total // (SIDE * SIDE)
    mid = wr.shape[1]
    band = count * SIDE
    waits[0]()
    reduced = jnp.maximum(dot(x, wr[...]), 0.0)
    reduced = reduced.reshape(count, SIDE, SIDE, mid).swapaxes(0, 1).reshape(band, SIDE, mid)
    taps = jnp.concatenate([p.reshape(total, mid).astype(BF16) for p in neighbours(reduced)], axis=1)
    waits[1]()
    edge = jnp.zeros((band, mid), F32)
    summed = dot(taps, ws[1])
    summed = summed + jnp.concatenate([edge, dot(taps[:-band], ws[0])], axis=0)
    summed = summed + jnp.concatenate([dot(taps[band:], ws[2]), edge], axis=0)
    spatial = jnp.maximum(summed, 0.0).reshape(SIDE, count, SIDE, mid).swapaxes(0, 1)
    spatial = spatial.reshape(total, mid).astype(BF16)
    waits[2]()
    out = jnp.maximum(dot(spatial, we[...]) + x.astype(F32), 0.0)
    return jnp.sum(out.reshape(count, SIDE * SIDE, x.shape[1]), axis=1) * (1.0 / (SIDE * SIDE))


def encode_kernel(x, wr_hbm, ws_hbm, we_hbm, wm_hbm, emb, wr, ws, we, wm, pooled, sems):
    step = pl.program_id(0)
    last = pl.num_programs(0) - 1
    copies = [
        pltpu.make_async_copy(src, dst, sems.at[i])
        for i, (src, dst) in enumerate(((wr_hbm, wr), (ws_hbm, ws), (we_hbm, we), (wm_hbm, wm)))
    ]

    def run(waits):
        count = x.shape[0] // (SIDE * SIDE)
        value = bottleneck(x[...], wr, ws, we, waits)
        pooled[pl.ds(pl.multiple_of(step * count, count), count), :] = value

    @pl.when(step == 0)
    def _():
        for copy in copies:
            copy.start()
        run([copy.wait for copy in copies])

    @pl.when(step > 0)
    def _():
        run([lambda: None] * 3)

    @pl.when(step == last)
    def _():
        copies[3].wait()
        emb[...] = dot(pooled[...].astype(BF16), wm[...]).astype(BF16)


def encode(flat, wr, ws, we, wm):
    total, c = flat.shape
    count = total // (SIDE * SIDE)
    rows = GROUP * SIDE * SIDE
    anywhere = pl.BlockSpec(memory_space=pl.ANY)
    return pl.pallas_call(
        encode_kernel,
        grid=(count // GROUP,),
        in_specs=[pl.BlockSpec((rows, c), lambda i: (i, 0))] + [anywhere] * 4,
        out_specs=pl.BlockSpec((count, wm.shape[1]), lambda i: (0, 0)),
        out_shape=jax.ShapeDtypeStruct((count, wm.shape[1]), BF16),
        scratch_shapes=[
            pltpu.VMEM(wr.shape, BF16),
            pltpu.VMEM(ws.shape, BF16),
            pltpu.VMEM(we.shape, BF16),
            pltpu.VMEM(wm.shape, BF16),
            pltpu.VMEM((count, c), F32),
            pltpu.SemaphoreType.DMA((4,)),
        ],
        compiler_params=pltpu.CompilerParams(vmem_limit_bytes=56 << 20),
        cost_estimate=pl.CostEstimate(
            flops=2 * total * (2 * c * wr.shape[1] + 9 * wr.shape[1] ** 2),
            bytes_accessed=2 * (total * c + wr.size + ws.size + we.size + wm.size),
            transcendentals=0,
        ),
        name="encode",
    )(flat, wr, ws, we, wm)


def project_kernel(heads, spread_of, emb, wq, wk, wv, *outs):
    a = lax.axis_index("blk") // spread_of
    scratch = outs[-1]
    rows = emb.shape[0]
    values = emb[...].astype(F32)
    center = jnp.mean(values, axis=1, keepdims=True)
    values = values - center
    spread = jnp.mean(values * values, axis=1, keepdims=True)
    normed = (values * lax.rsqrt(spread + 1e-05)).astype(BF16)
    query, key, value = (dot(normed, w[...]) for w in (wq, wk, wv))
    for head in range(heads):
        q, k, v = (r[:, head * HD : (head + 1) * HD] for r in (query, key, value))
        first = jnp.concatenate([q, v[:, 2 * THIRD :]], axis=1)
        second = jnp.concatenate([k, v[:, THIRD : 2 * THIRD]], axis=1)
        quarter = rows // 4
        third = jnp.concatenate([v[i * quarter : (i + 1) * quarter, :THIRD] for i in range(4)], axis=1)
        scratch[head] = jnp.concatenate([first, second, third], axis=0).astype(BF16)
    for e in range(heads):
        outs[e][...] = scratch[a ^ e]


def project(emb, wq, wk, wv, heads, spread_of):
    rows = emb.shape[0]
    packed = 2 * rows + rows // 4
    return pl.pallas_call(
        functools.partial(project_kernel, heads, spread_of),
        out_shape=[jax.ShapeDtypeStruct((packed, LANES), BF16)] * heads,
        scratch_shapes=[pltpu.VMEM((heads, packed, LANES), BF16)],
        compiler_params=pltpu.CompilerParams(vmem_limit_bytes=24 << 20),
        name="project",
    )(emb, wq, wk, wv)


def unpack_kernel(heads, *refs):
    own, out = refs[:heads], refs[heads]
    rows = own[0].shape[0] * 4 // 9
    quarter = rows // 4
    lane = lax.broadcasted_iota(jnp.int32, (rows, LANES), 1)
    for e in range(heads):
        first = own[e][:rows].astype(F32)
        second = own[e][rows : 2 * rows].astype(F32)
        third = own[e][2 * rows :].astype(F32)
        low = jnp.concatenate(
            [third] + [pltpu.roll(third, LANES - i * THIRD, axis=1) for i in range(1, 4)], axis=0
        )
        middle = pltpu.roll(second, 2 * THIRD, axis=1)
        high = pltpu.roll(first, 3 * THIRD, axis=1)
        value = jnp.where(lane < THIRD, low, jnp.where(lane < 2 * THIRD, middle, high))
        value = jnp.where(lane < HD, value, jnp.where(lane == HD, 1.0, 0.0))
        key = jnp.where(lane < HD, second, 0.0)
        out[e * rows : (e + 1) * rows, :LANES] = key.astype(BF16)
        out[e * rows : (e + 1) * rows, LANES:] = value.astype(BF16)


def unpack(own):
    rows = own[0].shape[0] * 4 // 9
    return pl.pallas_call(
        functools.partial(unpack_kernel, len(own)),
        out_shape=jax.ShapeDtypeStruct((len(own) * rows, 2 * LANES), BF16),
        compiler_params=pltpu.CompilerParams(vmem_limit_bytes=24 << 20),
        name="unpack",
    )(*own)


def attend_kernel(heads, spread_of, tiles_of, slide_tiles, *refs):
    own = refs[:heads]
    sets = refs[heads : heads + spread_of]
    out = refs[heads + spread_of]
    blk = lax.axis_index("blk")
    a, c = blk // spread_of, lax.rem(blk, spread_of)
    length = sets[0].shape[0] // heads
    count = length // tiles_of
    ends = [slide_tiles[0], slide_tiles[0] + slide_tiles[1]]
    ends.append(ends[1] + slide_tiles[2])

    def slide_of(shape, dim, start):
        pos = lax.broadcasted_iota(jnp.int32, shape, dim) + start
        return sum((pos >= end).astype(jnp.int32) for end in ends)

    key_slides = [
        jnp.concatenate(
            [slide_of((1, length), 1, ((a ^ e) * spread_of + (c ^ f)) * length) for e in range(heads)],
            axis=1,
        )
        for f in range(spread_of)
    ]
    scale = math.log2(math.e) / math.sqrt(HD)
    for e in range(heads):
        query = own[e][:length]
        query_slide = slide_of((length, 1), 0, ((a ^ e) * spread_of + c) * length)
        scores = []
        for f in range(spread_of):
            part = lax.dot_general(
                query, sets[f][:, :LANES], (((1,), (1,)), ((), ())), preferred_element_type=F32
            )
            scores.append(jnp.where(query_slide == key_slides[f], part, -1e30))
        top = functools.reduce(jnp.maximum, [jnp.max(s, axis=1, keepdims=True) for s in scores])
        product = sum(
            dot(jnp.exp2((s - top) * scale).astype(BF16), sets[f][:, LANES:])
            for f, s in enumerate(scores)
        )
        result = (product / product[:, HD : HD + 1]).astype(BF16)
        for t in range(tiles_of):
            out[t * heads + (a ^ e)] = result[t * count : (t + 1) * count]


def attend(slide_tiles, own, sets, tiles_of):
    heads, spread_of = len(own), len(sets)
    length = sets[0].shape[0] // heads
    whole = pl.BlockSpec(memory_space=pltpu.VMEM)
    return pl.pallas_call(
        functools.partial(attend_kernel, heads, spread_of, tiles_of),
        in_specs=[pl.BlockSpec(memory_space=pltpu.SMEM)] + [whole] * (heads + spread_of),
        out_specs=whole,
        out_shape=jax.ShapeDtypeStruct((tiles_of * heads, length // tiles_of, LANES), BF16),
        compiler_params=pltpu.CompilerParams(vmem_limit_bytes=40 << 20),
        name="attend",
    )(slide_tiles, *own, *sets)


def finish_kernel(heads, order, parts, emb, *refs):
    out = refs[-1]
    total = emb[...].astype(F32)
    for where, w in zip(order(), refs[:-1]):
        attended = jnp.concatenate(
            [parts[where * heads + h][:, :HD].astype(F32) for h in range(w.shape[0] // HD)], axis=1
        )
        total = total + dot(attended.astype(BF16), w[...])
    out[...] = total.astype(BF16)


def finish(parts, emb, w_outs, heads, order):
    return pl.pallas_call(
        functools.partial(finish_kernel, heads, order),
        out_shape=jax.ShapeDtypeStruct(emb.shape, BF16),
        compiler_params=pltpu.CompilerParams(vmem_limit_bytes=24 << 20),
        name="finish",
    )(parts, emb, *w_outs)


def fetch(x, flip, tiles_of, blks):
    pairs = [(t * blks + b, (t ^ flip[b % 2]) * blks + b) for t in range(tiles_of) for b in range(blks)]
    return lax.ppermute(x, ("tile", "blk"), pairs)


def tile_order():
    t, core = lax.axis_index("tile"), lax.rem(lax.axis_index("blk"), 2)
    return t, t ^ (1 + core), t ^ (2 - core), t ^ 3


def shards(tiles_of, blks, tiles, wr, ws, we, wm, wq, wk, wv, wo, slide_tiles):
    count = tiles.shape[0]
    flat = tiles.reshape(count * SIDE * SIDE, tiles.shape[3])
    mid = wr.shape[1]
    heads = wq.shape[1] // HD
    spread_of = blks // heads
    relay = tiles_of == 4
    first = fetch(wo, (1, 2), tiles_of, blks) if relay else lax.all_gather(wo, "tile", axis=0, tiled=True)
    emb = encode(flat, wr, ws.reshape(3, 3 * mid, mid), we, wm)
    gathered = lax.all_gather(emb, "tile", axis=0, tiled=True)
    mine = project(gathered, wq, wk, wv, heads, spread_of)
    own = [mine[0]]
    for e in range(1, heads):
        pairs = [(i, i ^ (e * spread_of)) for i in range(blks)]
        own.append(lax.ppermute(mine[e], "blk", pairs))
    if relay:
        first, *_ = lax.optimization_barrier((first, *own))
        second = lax.ppermute(first, "blk", [(b, b ^ 1) for b in range(blks)])
        third = fetch(first, (2, 1), tiles_of, blks)
        w_outs, order = [wo, first, second, third], tile_order
    else:
        w_outs, order = [first], lambda: (0,)
    sets = [unpack(own)]
    for f in range(1, spread_of):
        sets.append(lax.ppermute(sets[0], "blk", [(i, i ^ f) for i in range(blks)]))
    attended = attend(slide_tiles, own, sets, tiles_of)
    groups = [
        [t * blks + a * spread_of + c for t in range(tiles_of) for a in range(heads)]
        for c in range(spread_of)
    ]
    parts = lax.all_to_all(attended, ("tile", "blk"), 0, 0, axis_index_groups=groups, tiled=True)
    return finish(parts, emb, w_outs, heads, order)


def solution(mesh):
    placed = (
        P(("blk", "tile"), None, None, None),
        P(),
        P(),
        P(),
        P(),
        P(None, "tile"),
        P(None, "tile"),
        P(None, "tile"),
        P("tile", None),
        P(),
    )
    return jax.shard_map(
        functools.partial(shards, mesh.shape["tile"], mesh.shape["blk"]),
        mesh=mesh,
        in_specs=placed,
        out_specs=P(("blk", "tile"), None),
        check_vma=False,
    )
```

```python
import functools
import math

import jax
import jax.numpy as jnp
from jax import lax
from jax.experimental import pallas as pl
from jax.experimental.pallas import tpu as pltpu
from jax.sharding import PartitionSpec as P

SIDE = 8
HD = 96
THIRD = HD // 3
LANES = 128
F32 = jnp.float32
BF16 = jnp.bfloat16
GROUP = 16
PART = 8


def dot(a, b):
    return jnp.dot(a, b, preferred_element_type=F32)


def neighbours(rows):
    col = lax.broadcasted_iota(jnp.int32, rows.shape, 1)
    left = jnp.where(col >= 1, pltpu.roll(rows, 1, axis=1), 0.0)
    right = jnp.where(col <= SIDE - 2, pltpu.roll(rows, SIDE - 1, axis=1), 0.0)
    return left, rows, right


def row_combinations(d):
    even, odd = d[4] - 4.0 * d[2], d[3] - 4.0 * d[1]
    even2, odd2 = d[4] - d[2], 2.0 * (d[3] - d[1])
    return (
        d[0] - 1.25 * d[2] + 0.25 * d[4],
        even + odd,
        even - odd,
        even2 + odd2,
        even2 - odd2,
        4.0 * d[1] - 5.0 * d[3] + d[5],
    )


def tap_combinations(g):
    near, far = g[0] + g[2], g[0] + g[2] * 4
    double = g[1] * 2
    return near + g[1], near - g[1], far + double, far - double


def four_rows(m):
    near, near_odd = (m[1] + m[2]) * (-1 / 6), (m[1] - m[2]) * (-1 / 6)
    far, far_odd = (m[3] + m[4]) * (1 / 24), (m[3] - m[4]) * (1 / 24)
    return (
        m[0] + near + far,
        near_odd + 2.0 * far_odd,
        near + 4.0 * far,
        near_odd + 8.0 * far_odd + m[5],
    )


def encode_kernel(
    x_hbm, wr_hbm, ws_hbm, we_hbm, wm_hbm, emb,
    x, wr, ws, we, wm, mixed_taps, reduced, products, pooled, x_sems, tap_sems, sems,
):
    step = pl.program_id(0)
    count, c = pooled.shape
    area = SIDE * SIDE
    mid = wr.shape[1]
    groups = count // GROUP
    per = GROUP // PART
    parts = groups * per
    chunk = 3 * mid // parts

    def x_copy(g):
        at = pl.ds(pl.multiple_of(g * PART * area, PART * area), PART * area)
        return pltpu.make_async_copy(x_hbm.at[at], x.at[at], x_sems.at[g])

    def tap_copy(g):
        at = pl.ds(pl.multiple_of(g * chunk, chunk), chunk)
        return pltpu.make_async_copy(ws_hbm.at[:, at], ws.at[:, at], tap_sems.at[g])

    wr_copy, we_copy, wm_copy = (
        pltpu.make_async_copy(src, dst, sems.at[i])
        for i, (src, dst) in enumerate(((wr_hbm, wr), (we_hbm, we), (wm_hbm, wm)))
    )

    @pl.when(step == 0)
    def _():
        x_copy(0).start()
        wr_copy.start()
        x_copy(1).start()
        wr_copy.wait()
        tap_copy(0).start()
        tap_copy(1).start()

    @pl.when(step < groups)
    def _():
        for i in range(per):
            g = step * per + i
            x_copy(g).wait()

            @pl.when(g + 2 < parts)
            def _():
                x_copy(g + 2).start()
                tap_copy(g + 2).start()

            rows = x[pl.ds(pl.multiple_of(g * PART * area, PART * area), PART * area), :]
            maps = jnp.maximum(dot(rows, wr[...]), 0.0).reshape(PART, SIDE, SIDE, mid)
            reduced[:, pl.ds(pl.multiple_of(g * PART, PART), PART)] = maps.swapaxes(0, 1)
            tap_copy(g).wait()
            at = pl.ds(pl.multiple_of(g * chunk, chunk), chunk)
            for k, taps in enumerate(tap_combinations([ws[dy, at, :] for dy in range(3)])):
                mixed_taps[k, at, :] = taps

    @pl.when(step == groups - 1)
    def _():
        we_copy.start()

    @pl.when(step == groups)
    def _():
        wm_copy.start()
        we_copy.wait()

    @pl.when(step >= groups)
    def _():
        g = step - groups
        band = GROUP * SIDE
        maps = reduced[:, pl.ds(pl.multiple_of(g * GROUP, GROUP), GROUP)].reshape(SIDE, band, mid)
        edge = jnp.zeros((band, mid), F32)
        d = [edge] + [maps[i] for i in range(SIDE)] + [edge]
        upper, lower = row_combinations(d[0:6]), row_combinations(d[4:10])
        taps = [ws.at[0]] + [mixed_taps.at[k] for k in range(4)] + [ws.at[2]]
        for k in range(6):
            both = jnp.concatenate([upper[k], lower[k]], axis=0).reshape(2 * GROUP, SIDE, mid)
            window = [p.reshape(2 * band, mid).astype(BF16) for p in neighbours(both)]
            products[k] = dot(jnp.concatenate(window, axis=1), taps[k][...])
        rows = four_rows([products[k, :band] for k in range(6)])
        rows += four_rows([products[k, band:] for k in range(6)])
        spatial = jnp.stack([jnp.maximum(r, 0.0).reshape(GROUP, SIDE, mid) for r in rows], axis=0)
        spatial = spatial.swapaxes(0, 1).reshape(GROUP * area, mid).astype(BF16)
        at = pl.ds(pl.multiple_of(g * GROUP * area, GROUP * area), GROUP * area)
        out = jnp.maximum(dot(spatial, we[...]) + x[at, :].astype(F32), 0.0)
        mean = jnp.sum(out.reshape(GROUP, area, c), axis=1) * (1.0 / area)
        pooled[pl.ds(pl.multiple_of(g * GROUP, GROUP), GROUP), :] = mean

    @pl.when(step == 2 * groups - 1)
    def _():
        wm_copy.wait()
        emb[...] = dot(pooled[...].astype(BF16), wm[...]).astype(BF16)


def encode(flat, wr, ws, we, wm):
    total, c = flat.shape
    count = total // (SIDE * SIDE)
    mid = wr.shape[1]
    return pl.pallas_call(
        encode_kernel,
        grid=(2 * count // GROUP,),
        in_specs=[pl.BlockSpec(memory_space=pl.ANY)] * 5,
        out_specs=pl.BlockSpec((count, wm.shape[1]), lambda i: (0, 0)),
        out_shape=jax.ShapeDtypeStruct((count, wm.shape[1]), BF16),
        scratch_shapes=[
            pltpu.VMEM(flat.shape, BF16),
            pltpu.VMEM(wr.shape, BF16),
            pltpu.VMEM(ws.shape, BF16),
            pltpu.VMEM(we.shape, BF16),
            pltpu.VMEM(wm.shape, BF16),
            pltpu.VMEM((4,) + ws.shape[1:], BF16),
            pltpu.VMEM((SIDE, count, SIDE, mid), F32),
            pltpu.VMEM((6, 2 * GROUP * SIDE, mid), F32),
            pltpu.VMEM((count, c), F32),
            pltpu.SemaphoreType.DMA((count // PART,)),
            pltpu.SemaphoreType.DMA((count // PART,)),
            pltpu.SemaphoreType.DMA((3,)),
        ],
        compiler_params=pltpu.CompilerParams(vmem_limit_bytes=62 << 20),
        cost_estimate=pl.CostEstimate(
            flops=2 * total * (2 * c * mid + 9 * mid**2),
            bytes_accessed=2 * (total * c + wr.size + ws.size + we.size + wm.size),
            transcendentals=0,
        ),
        name="encode",
    )(flat, wr, ws, we, wm)


def project_kernel(heads, spread_of, emb, wq, wk, wv, *outs):
    a = lax.axis_index("blk") // spread_of
    scratch = outs[-1]
    rows = emb.shape[0]
    values = emb[...].astype(F32)
    center = jnp.mean(values, axis=1, keepdims=True)
    values = values - center
    spread = jnp.mean(values * values, axis=1, keepdims=True)
    normed = (values * lax.rsqrt(spread + 1e-05)).astype(BF16)
    query, key, value = (dot(normed, w[...]) for w in (wq, wk, wv))
    for head in range(heads):
        q, k, v = (r[:, head * HD : (head + 1) * HD] for r in (query, key, value))
        first = jnp.concatenate([q, v[:, 2 * THIRD :]], axis=1)
        second = jnp.concatenate([k, v[:, THIRD : 2 * THIRD]], axis=1)
        quarter = rows // 4
        third = jnp.concatenate([v[i * quarter : (i + 1) * quarter, :THIRD] for i in range(4)], axis=1)
        scratch[head] = jnp.concatenate([first, second, third], axis=0).astype(BF16)
    for e in range(heads):
        outs[e][...] = scratch[a ^ e]


def project(emb, wq, wk, wv, heads, spread_of):
    rows = emb.shape[0]
    packed = 2 * rows + rows // 4
    return pl.pallas_call(
        functools.partial(project_kernel, heads, spread_of),
        out_shape=[jax.ShapeDtypeStruct((packed, LANES), BF16)] * heads,
        scratch_shapes=[pltpu.VMEM((heads, packed, LANES), BF16)],
        compiler_params=pltpu.CompilerParams(vmem_limit_bytes=24 << 20),
        name="project",
    )(emb, wq, wk, wv)


def unpack_kernel(heads, *refs):
    own, out = refs[:heads], refs[heads]
    rows = own[0].shape[0] * 4 // 9
    quarter = rows // 4
    lane = lax.broadcasted_iota(jnp.int32, (rows, LANES), 1)
    for e in range(heads):
        first = own[e][:rows].astype(F32)
        second = own[e][rows : 2 * rows].astype(F32)
        third = own[e][2 * rows :].astype(F32)
        low = jnp.concatenate(
            [third] + [pltpu.roll(third, LANES - i * THIRD, axis=1) for i in range(1, 4)], axis=0
        )
        middle = pltpu.roll(second, 2 * THIRD, axis=1)
        high = pltpu.roll(first, 3 * THIRD, axis=1)
        value = jnp.where(lane < THIRD, low, jnp.where(lane < 2 * THIRD, middle, high))
        value = jnp.where(lane < HD, value, jnp.where(lane == HD, 1.0, 0.0))
        key = jnp.where(lane < HD, second, 0.0)
        out[e * rows : (e + 1) * rows, :LANES] = key.astype(BF16)
        out[e * rows : (e + 1) * rows, LANES:] = value.astype(BF16)


def unpack(own):
    rows = own[0].shape[0] * 4 // 9
    return pl.pallas_call(
        functools.partial(unpack_kernel, len(own)),
        out_shape=jax.ShapeDtypeStruct((len(own) * rows, 2 * LANES), BF16),
        compiler_params=pltpu.CompilerParams(vmem_limit_bytes=24 << 20),
        name="unpack",
    )(*own)


def attend_kernel(heads, spread_of, tiles_of, slide_tiles, *refs):
    own = refs[:heads]
    sets = refs[heads : heads + spread_of]
    out = refs[heads + spread_of]
    blk = lax.axis_index("blk")
    a, c = blk // spread_of, lax.rem(blk, spread_of)
    length = sets[0].shape[0] // heads
    count = length // tiles_of
    ends = [slide_tiles[0], slide_tiles[0] + slide_tiles[1]]
    ends.append(ends[1] + slide_tiles[2])

    def slide_of(shape, dim, start):
        pos = lax.broadcasted_iota(jnp.int32, shape, dim) + start
        return sum((pos >= end).astype(jnp.int32) for end in ends)

    key_slides = [
        jnp.concatenate(
            [slide_of((1, length), 1, ((a ^ e) * spread_of + (c ^ f)) * length) for e in range(heads)],
            axis=1,
        )
        for f in range(spread_of)
    ]
    scale = math.log2(math.e) / math.sqrt(HD)
    for e in range(heads):
        query = own[e][:length]
        query_slide = slide_of((length, 1), 0, ((a ^ e) * spread_of + c) * length)
        scores = []
        for f in range(spread_of):
            part = lax.dot_general(
                query, sets[f][:, :LANES], (((1,), (1,)), ((), ())), preferred_element_type=F32
            )
            scores.append(jnp.where(query_slide == key_slides[f], part, -1e30))
        top = functools.reduce(jnp.maximum, [jnp.max(s, axis=1, keepdims=True) for s in scores])
        product = sum(
            dot(jnp.exp2((s - top) * scale).astype(BF16), sets[f][:, LANES:])
            for f, s in enumerate(scores)
        )
        result = (product / product[:, HD : HD + 1]).astype(BF16)
        for t in range(tiles_of):
            out[t * heads + (a ^ e)] = result[t * count : (t + 1) * count]


def attend(slide_tiles, own, sets, tiles_of):
    heads, spread_of = len(own), len(sets)
    length = sets[0].shape[0] // heads
    whole = pl.BlockSpec(memory_space=pltpu.VMEM)
    return pl.pallas_call(
        functools.partial(attend_kernel, heads, spread_of, tiles_of),
        in_specs=[pl.BlockSpec(memory_space=pltpu.SMEM)] + [whole] * (heads + spread_of),
        out_specs=whole,
        out_shape=jax.ShapeDtypeStruct((tiles_of * heads, length // tiles_of, LANES), BF16),
        compiler_params=pltpu.CompilerParams(vmem_limit_bytes=40 << 20),
        name="attend",
    )(slide_tiles, *own, *sets)


def finish_kernel(heads, order, parts, emb, *refs):
    out = refs[-1]
    total = emb[...].astype(F32)
    for where, w in zip(order(), refs[:-1]):
        attended = jnp.concatenate(
            [parts[where * heads + h][:, :HD].astype(F32) for h in range(w.shape[0] // HD)], axis=1
        )
        total = total + dot(attended.astype(BF16), w[...])
    out[...] = total.astype(BF16)


def finish(parts, emb, w_outs, heads, order):
    return pl.pallas_call(
        functools.partial(finish_kernel, heads, order),
        out_shape=jax.ShapeDtypeStruct(emb.shape, BF16),
        compiler_params=pltpu.CompilerParams(vmem_limit_bytes=24 << 20),
        name="finish",
    )(parts, emb, *w_outs)


def fetch(x, flip, tiles_of, blks):
    pairs = [(t * blks + b, (t ^ flip[b % 2]) * blks + b) for t in range(tiles_of) for b in range(blks)]
    return lax.ppermute(x, ("tile", "blk"), pairs)


def tile_order():
    t, core = lax.axis_index("tile"), lax.rem(lax.axis_index("blk"), 2)
    return t, t ^ (1 + core), t ^ (2 - core), t ^ 3


def shards(tiles_of, blks, tiles, wr, ws, we, wm, wq, wk, wv, wo, slide_tiles):
    count = tiles.shape[0]
    flat = tiles.reshape(count * SIDE * SIDE, tiles.shape[3])
    mid = wr.shape[1]
    heads = wq.shape[1] // HD
    spread_of = blks // heads
    relay = tiles_of == 4
    first = fetch(wo, (1, 2), tiles_of, blks) if relay else lax.all_gather(wo, "tile", axis=0, tiled=True)
    emb = encode(flat, wr, ws.reshape(3, 3 * mid, mid), we, wm)
    gathered = lax.all_gather(emb, "tile", axis=0, tiled=True)
    mine = project(gathered, wq, wk, wv, heads, spread_of)
    own = [mine[0]]
    for e in range(1, heads):
        pairs = [(i, i ^ (e * spread_of)) for i in range(blks)]
        own.append(lax.ppermute(mine[e], "blk", pairs))
    if relay:
        first, *_ = lax.optimization_barrier((first, *own))
        second = lax.ppermute(first, "blk", [(b, b ^ 1) for b in range(blks)])
        third = fetch(first, (2, 1), tiles_of, blks)
        w_outs, order = [wo, first, second, third], tile_order
    else:
        w_outs, order = [first], lambda: (0,)
    sets = [unpack(own)]
    for f in range(1, spread_of):
        sets.append(lax.ppermute(sets[0], "blk", [(i, i ^ f) for i in range(blks)]))
    attended = attend(slide_tiles, own, sets, tiles_of)
    groups = [
        [t * blks + a * spread_of + c for t in range(tiles_of) for a in range(heads)]
        for c in range(spread_of)
    ]
    parts = lax.all_to_all(attended, ("tile", "blk"), 0, 0, axis_index_groups=groups, tiled=True)
    return finish(parts, emb, w_outs, heads, order)


def solution(mesh):
    placed = (
        P(("blk", "tile"), None, None, None),
        P(),
        P(),
        P(),
        P(),
        P(None, "tile"),
        P(None, "tile"),
        P(None, "tile"),
        P("tile", None),
        P(),
    )
    return jax.shard_map(
        functools.partial(shards, mesh.shape["tile"], mesh.shape["blk"]),
        mesh=mesh,
        in_specs=placed,
        out_specs=P(("blk", "tile"), None),
        check_vma=False,
    )
```

```python
import functools
import math

import jax
import jax.numpy as jnp
from jax import lax
from jax.experimental import pallas as pl
from jax.experimental.pallas import tpu as pltpu
from jax.sharding import PartitionSpec as P

SIDE = 8
HD = 96
THIRD = HD // 3
LANES = 128
F32 = jnp.float32
BF16 = jnp.bfloat16
GROUP = 16
PART = 8


def dot(a, b):
    return jnp.dot(a, b, preferred_element_type=F32)


def neighbours(rows):
    col = lax.broadcasted_iota(jnp.int32, rows.shape, 1)
    left = jnp.where(col >= 1, pltpu.roll(rows, 1, axis=1), 0.0)
    right = jnp.where(col <= SIDE - 2, pltpu.roll(rows, SIDE - 1, axis=1), 0.0)
    return left, rows, right


def row_combinations(d):
    even, odd = d[4] - 4.0 * d[2], d[3] - 4.0 * d[1]
    even2, odd2 = d[4] - d[2], 2.0 * (d[3] - d[1])
    return (
        d[0] - 1.25 * d[2] + 0.25 * d[4],
        even + odd,
        even - odd,
        even2 + odd2,
        even2 - odd2,
        4.0 * d[1] - 5.0 * d[3] + d[5],
    )


def tap_combinations(g):
    near, far = g[0] + g[2], g[0] + g[2] * 4
    double = g[1] * 2
    return near + g[1], near - g[1], far + double, far - double


def four_rows(m):
    near, near_odd = (m[1] + m[2]) * (-1 / 6), (m[1] - m[2]) * (-1 / 6)
    far, far_odd = (m[3] + m[4]) * (1 / 24), (m[3] - m[4]) * (1 / 24)
    return (
        m[0] + near + far,
        near_odd + 2.0 * far_odd,
        near + 4.0 * far,
        near_odd + 8.0 * far_odd + m[5],
    )


def encode_kernel(
    x_hbm, wr_hbm, ws_hbm, we_hbm, wm_hbm, emb,
    x, wr, ws, we, mixed_taps, reduced, products, pooled, x_sems, tap_sems, sems,
):
    step = pl.program_id(0)
    count, c = pooled.shape
    area = SIDE * SIDE
    mid = wr.shape[1]
    groups = count // GROUP
    per = GROUP // PART
    parts = groups * per
    chunk = 3 * mid // parts

    def x_copy(g):
        at = pl.ds(pl.multiple_of(g * PART * area, PART * area), PART * area)
        return pltpu.make_async_copy(x_hbm.at[at], x.at[at], x_sems.at[g])

    def tap_copy(g):
        at = pl.ds(pl.multiple_of(g * chunk, chunk), chunk)
        return pltpu.make_async_copy(ws_hbm.at[:, at], ws.at[:, at], tap_sems.at[g])

    wm = x.at[: wm_hbm.shape[0], : wm_hbm.shape[1]]
    wr_copy, we_copy, wm_copy = (
        pltpu.make_async_copy(src, dst, sems.at[i])
        for i, (src, dst) in enumerate(((wr_hbm, wr), (we_hbm, we), (wm_hbm, wm)))
    )

    @pl.when(step == 0)
    def _():
        x_copy(0).start()
        wr_copy.start()
        x_copy(1).start()
        wr_copy.wait()
        tap_copy(0).start()
        tap_copy(1).start()

    @pl.when(step < groups)
    def _():
        for i in range(per):
            g = step * per + i
            x_copy(g).wait()

            @pl.when(g + 2 < parts)
            def _():
                x_copy(g + 2).start()
                tap_copy(g + 2).start()

            rows = x[pl.ds(pl.multiple_of(g * PART * area, PART * area), PART * area), :]
            maps = jnp.maximum(dot(rows, wr[...]), 0.0).reshape(PART, SIDE, SIDE, mid)
            reduced[:, pl.ds(pl.multiple_of(g * PART, PART), PART)] = maps.swapaxes(0, 1)
            tap_copy(g).wait()
            at = pl.ds(pl.multiple_of(g * chunk, chunk), chunk)
            for k, taps in enumerate(tap_combinations([ws[dy, at, :] for dy in range(3)])):
                mixed_taps[k, at, :] = taps

    @pl.when(step == groups - 1)
    def _():
        we_copy.start()

    @pl.when(step == groups)
    def _():
        we_copy.wait()

    @pl.when(step == 2 * groups - 1)
    def _():
        wm_copy.start()

    @pl.when(step >= groups)
    def _():
        g = step - groups
        band = GROUP * SIDE
        maps = reduced[:, pl.ds(pl.multiple_of(g * GROUP, GROUP), GROUP)].reshape(SIDE, band, mid)
        edge = jnp.zeros((band, mid), F32)
        d = [edge] + [maps[i] for i in range(SIDE)] + [edge]
        upper, lower = row_combinations(d[0:6]), row_combinations(d[4:10])
        taps = [ws.at[0]] + [mixed_taps.at[k] for k in range(4)] + [ws.at[2]]
        for k in range(6):
            both = jnp.concatenate([upper[k], lower[k]], axis=0).reshape(2 * GROUP, SIDE, mid)
            window = [p.reshape(2 * band, mid).astype(BF16) for p in neighbours(both)]
            products[k] = dot(jnp.concatenate(window, axis=1), taps[k][...])
        rows = four_rows([products[k, :band] for k in range(6)])
        rows += four_rows([products[k, band:] for k in range(6)])
        spatial = jnp.stack([jnp.maximum(r, 0.0).reshape(GROUP, SIDE, mid) for r in rows], axis=0)
        spatial = spatial.swapaxes(0, 1).reshape(GROUP * area, mid).astype(BF16)
        at = pl.ds(pl.multiple_of(g * GROUP * area, GROUP * area), GROUP * area)
        out = jnp.maximum(dot(spatial, we[...]) + x[at, :].astype(F32), 0.0)
        mean = jnp.sum(out.reshape(GROUP, area, c), axis=1) * (1.0 / area)
        pooled[pl.ds(pl.multiple_of(g * GROUP, GROUP), GROUP), :] = mean

    @pl.when(step == 2 * groups - 1)
    def _():
        wm_copy.wait()
        emb[...] = dot(pooled[...].astype(BF16), wm[...]).astype(BF16)


def encode(flat, wr, ws, we, wm):
    total, c = flat.shape
    count = total // (SIDE * SIDE)
    assert wm.shape[0] <= total - GROUP * SIDE * SIDE and wm.shape[1] <= c
    mid = wr.shape[1]
    return pl.pallas_call(
        encode_kernel,
        grid=(2 * count // GROUP,),
        in_specs=[pl.BlockSpec(memory_space=pl.ANY)] * 5,
        out_specs=pl.BlockSpec((count, wm.shape[1]), lambda i: (0, 0)),
        out_shape=jax.ShapeDtypeStruct((count, wm.shape[1]), BF16),
        scratch_shapes=[
            pltpu.VMEM(flat.shape, BF16),
            pltpu.VMEM(wr.shape, BF16),
            pltpu.VMEM(ws.shape, BF16),
            pltpu.VMEM(we.shape, BF16),
            pltpu.VMEM((4,) + ws.shape[1:], BF16),
            pltpu.VMEM((SIDE, count, SIDE, mid), F32),
            pltpu.VMEM((6, 2 * GROUP * SIDE, mid), F32),
            pltpu.VMEM((count, c), F32),
            pltpu.SemaphoreType.DMA((count // PART,)),
            pltpu.SemaphoreType.DMA((count // PART,)),
            pltpu.SemaphoreType.DMA((3,)),
        ],
        compiler_params=pltpu.CompilerParams(vmem_limit_bytes=54 << 20),
        cost_estimate=pl.CostEstimate(
            flops=2 * total * (2 * c * mid + 9 * mid**2),
            bytes_accessed=2 * (total * c + wr.size + ws.size + we.size + wm.size),
            transcendentals=0,
        ),
        name="encode",
    )(flat, wr, ws, we, wm)


def project_kernel(heads, spread_of, emb, wq, wk, wv, *outs):
    a = lax.axis_index("blk") // spread_of
    scratch = outs[-1]
    rows = emb.shape[0]
    values = emb[...].astype(F32)
    center = jnp.mean(values, axis=1, keepdims=True)
    values = values - center
    spread = jnp.mean(values * values, axis=1, keepdims=True)
    normed = (values * lax.rsqrt(spread + 1e-05)).astype(BF16)
    query, key, value = (dot(normed, w[...]) for w in (wq, wk, wv))
    for head in range(heads):
        q, k, v = (r[:, head * HD : (head + 1) * HD] for r in (query, key, value))
        first = jnp.concatenate([q, v[:, 2 * THIRD :]], axis=1)
        second = jnp.concatenate([k, v[:, THIRD : 2 * THIRD]], axis=1)
        quarter = rows // 4
        third = jnp.concatenate([v[i * quarter : (i + 1) * quarter, :THIRD] for i in range(4)], axis=1)
        scratch[head] = jnp.concatenate([first, second, third], axis=0).astype(BF16)
    for e in range(heads):
        outs[e][...] = scratch[a ^ e]


def project(emb, wq, wk, wv, heads, spread_of):
    rows = emb.shape[0]
    packed = 2 * rows + rows // 4
    return pl.pallas_call(
        functools.partial(project_kernel, heads, spread_of),
        out_shape=[jax.ShapeDtypeStruct((packed, LANES), BF16)] * heads,
        scratch_shapes=[pltpu.VMEM((heads, packed, LANES), BF16)],
        compiler_params=pltpu.CompilerParams(vmem_limit_bytes=24 << 20),
        name="project",
    )(emb, wq, wk, wv)


def unpack_kernel(heads, *refs):
    own, out = refs[:heads], refs[heads]
    rows = own[0].shape[0] * 4 // 9
    quarter = rows // 4
    lane = lax.broadcasted_iota(jnp.int32, (rows, LANES), 1)
    for e in range(heads):
        first = own[e][:rows].astype(F32)
        second = own[e][rows : 2 * rows].astype(F32)
        third = own[e][2 * rows :].astype(F32)
        low = jnp.concatenate(
            [third] + [pltpu.roll(third, LANES - i * THIRD, axis=1) for i in range(1, 4)], axis=0
        )
        middle = pltpu.roll(second, 2 * THIRD, axis=1)
        high = pltpu.roll(first, 3 * THIRD, axis=1)
        value = jnp.where(lane < THIRD, low, jnp.where(lane < 2 * THIRD, middle, high))
        value = jnp.where(lane < HD, value, jnp.where(lane == HD, 1.0, 0.0))
        key = jnp.where(lane < HD, second, 0.0)
        out[e * rows : (e + 1) * rows, :LANES] = key.astype(BF16)
        out[e * rows : (e + 1) * rows, LANES:] = value.astype(BF16)


def unpack(own):
    rows = own[0].shape[0] * 4 // 9
    return pl.pallas_call(
        functools.partial(unpack_kernel, len(own)),
        out_shape=jax.ShapeDtypeStruct((len(own) * rows, 2 * LANES), BF16),
        compiler_params=pltpu.CompilerParams(vmem_limit_bytes=24 << 20),
        name="unpack",
    )(*own)


class Slides:
    def __init__(self, slide_tiles, heads, spread_of, length):
        blk = lax.axis_index("blk")
        self.a, self.c = blk // spread_of, lax.rem(blk, spread_of)
        self.heads, self.spread_of, self.length = heads, spread_of, length
        first = slide_tiles[0]
        second = first + slide_tiles[1]
        self.ends = (first, second, second + slide_tiles[2])

    def of(self, e, f, dim):
        shape = (self.length, 1) if dim == 0 else (1, self.length)
        start = ((self.a ^ e) * self.spread_of + (self.c ^ f)) * self.length
        pos = lax.broadcasted_iota(jnp.int32, shape, dim) + start
        return sum((pos >= end).astype(jnp.int32) for end in self.ends)

    def of_keys(self, f):
        return jnp.concatenate([self.of(e, f, 1) for e in range(self.heads)], axis=1)


SCALE = math.log2(math.e) / math.sqrt(HD)


def masked_scores(query, keys, query_slide, key_slide):
    scores = lax.dot_general(query, keys, (((1,), (1,)), ((), ())), preferred_element_type=F32)
    return jnp.where(query_slide == key_slide, scores, -1e30)


def attend_own_kernel(heads, spread_of, slide_tiles, *refs):
    own, key_value, out = refs[:heads], refs[heads], refs[heads + 1]
    length = key_value.shape[0] // heads
    slides = Slides(slide_tiles, heads, spread_of, length)
    key_slide = slides.of_keys(0)
    lane = lax.broadcasted_iota(jnp.int32, (length, LANES), 1)
    for e in range(heads):
        scores = masked_scores(own[e][:length], key_value[:, :LANES], slides.of(e, 0, 0), key_slide)
        top = jnp.max(scores, axis=1, keepdims=True)
        product = dot(jnp.exp2((scores - top) * SCALE).astype(BF16), key_value[:, LANES:])
        out[e] = jnp.where(lane == HD + 1, top, product)


def attend_others_kernel(heads, spread_of, slide_tiles, *refs):
    own, partial, others = refs[:heads], refs[heads], refs[heads + 1 : heads + spread_of]
    outs = refs[heads + spread_of :]
    length = partial.shape[1]
    slides = Slides(slide_tiles, heads, spread_of, length)
    key_slides = [slides.of_keys(f) for f in range(1, spread_of)]
    quarter = length // 4
    for e in range(heads):
        query_slide = slides.of(e, 0, 0)
        scores = [
            masked_scores(own[e][:length], other[:, :LANES], query_slide, key_slide)
            for other, key_slide in zip(others, key_slides)
        ]
        before = partial[e]
        top_before = before[:, HD + 1 : HD + 2]
        top = functools.reduce(
            jnp.maximum, [jnp.max(s, axis=1, keepdims=True) for s in scores], top_before
        )
        product = before * jnp.exp2((top_before - top) * SCALE)
        for other, s in zip(others, scores):
            product = product + dot(jnp.exp2((s - top) * SCALE).astype(BF16), other[:, LANES:])
        result = product[:, :HD] / product[:, HD : HD + 1]
        rest = result[3 * quarter :]
        rest = jnp.concatenate([rest[:, i * THIRD : (i + 1) * THIRD] for i in range(3)], axis=0)
        outs[e][...] = jnp.concatenate([result[: 3 * quarter], rest], axis=1).astype(BF16)


def attend(slide_tiles, own, key_value, exchange):
    heads = len(own)
    length = key_value.shape[0] // heads
    others = exchange(key_value)
    spread_of = len(others) + 1
    small = pl.BlockSpec(memory_space=pltpu.SMEM)
    whole = pl.BlockSpec(memory_space=pltpu.VMEM)
    params = pltpu.CompilerParams(vmem_limit_bytes=40 << 20)
    rows = length * heads
    cost = pl.CostEstimate(
        flops=4 * rows * rows * LANES, bytes_accessed=6 * rows * LANES, transcendentals=rows * rows
    )
    partial = pl.pallas_call(
        functools.partial(attend_own_kernel, heads, spread_of),
        in_specs=[small] + [whole] * (heads + 1),
        out_specs=whole,
        out_shape=jax.ShapeDtypeStruct((heads, length, LANES), F32),
        compiler_params=params,
        cost_estimate=cost,
        name="attend_own",
    )(slide_tiles, *own, key_value)
    return pl.pallas_call(
        functools.partial(attend_others_kernel, heads, spread_of),
        in_specs=[small] + [whole] * (heads + spread_of),
        out_specs=[whole] * heads,
        out_shape=[jax.ShapeDtypeStruct((length * 3 // 4, LANES), BF16)] * heads,
        compiler_params=params,
        name="attend_others",
    )(slide_tiles, *own, partial, *others)


def partial_out_kernel(heads, tiles_of, spread_of, *refs):
    parts, w_out, outs = refs[:heads], refs[heads], refs[heads + 1 : heads + 1 + tiles_of]
    sorted_heads, sums = refs[heads + 1 + tiles_of :]
    a, t = lax.axis_index("blk") // spread_of, lax.axis_index("tile")
    quarter = parts[0].shape[0] // 3
    for e in range(heads):
        packed = parts[e][...].astype(F32)
        tail = packed[:, HD:]
        rest = jnp.concatenate([tail[i * quarter : (i + 1) * quarter] for i in range(3)], axis=1)
        sorted_heads[a ^ e] = jnp.concatenate([packed[:, :HD], rest], axis=0)
    attended = jnp.concatenate([sorted_heads[h] for h in range(heads)], axis=1).astype(BF16)
    product = dot(attended, w_out[...])
    count = product.shape[0] // tiles_of
    for block in range(tiles_of):
        sums[block] = product[block * count : (block + 1) * count]
    for d in range(tiles_of):
        outs[d][...] = sums[t ^ d].astype(outs[d].dtype)


def partial_out(parts, w_out, tiles_of, spread_of):
    heads, width = len(parts), w_out.shape[1]
    length = parts[0].shape[0] * 4 // 3
    count = length // tiles_of
    whole = pl.BlockSpec(memory_space=pltpu.VMEM)
    return pl.pallas_call(
        functools.partial(partial_out_kernel, heads, tiles_of, spread_of),
        in_specs=[whole] * (heads + 1),
        out_specs=[whole] * tiles_of,
        out_shape=[jax.ShapeDtypeStruct((count, width), F32 if d == 0 else BF16) for d in range(tiles_of)],
        scratch_shapes=[pltpu.VMEM((heads, length, HD), F32), pltpu.VMEM((tiles_of, count, width), F32)],
        compiler_params=pltpu.CompilerParams(vmem_limit_bytes=24 << 20),
        name="partial_out",
    )(*parts, w_out)


def finish_kernel(emb, *refs):
    total = emb[...].astype(F32)
    for ref in refs[:-1]:
        total = total + ref[...].astype(F32)
    refs[-1][...] = total.astype(BF16)


def finish(emb, sums):
    return pl.pallas_call(
        finish_kernel,
        out_shape=jax.ShapeDtypeStruct(emb.shape, BF16),
        compiler_params=pltpu.CompilerParams(vmem_limit_bytes=24 << 20),
        name="finish",
    )(emb, *sums)


def shards(tiles_of, blks, tiles, wr, ws, we, wm, wq, wk, wv, wo, slide_tiles):
    count = tiles.shape[0]
    flat = tiles.reshape(count * SIDE * SIDE, tiles.shape[3])
    mid = wr.shape[1]
    heads = wq.shape[1] // HD
    spread_of = blks // heads

    def along(x, axis, size, step):
        return lax.ppermute(x, axis, [(i, i ^ step) for i in range(size)])

    def over_heads(blocks):
        return [blocks[0]] + [along(blocks[e], "blk", blks, e * spread_of) for e in range(1, heads)]

    emb = encode(flat, wr, ws.reshape(3, 3 * mid, mid), we, wm)
    gathered = lax.all_gather(emb, "tile", axis=0, tiled=True)
    own = over_heads(project(gathered, wq, wk, wv, heads, spread_of))
    attended = attend(
        slide_tiles, own, unpack(own), lambda x: [along(x, "blk", blks, f) for f in range(1, spread_of)]
    )
    sums = partial_out(over_heads(attended), wo, tiles_of, spread_of)
    sums = [sums[0]] + [along(sums[d], "tile", tiles_of, d) for d in range(1, tiles_of)]
    return finish(emb, sums)


def solution(mesh):
    placed = (
        P(("blk", "tile"), None, None, None),
        P(),
        P(),
        P(),
        P(),
        P(None, "tile"),
        P(None, "tile"),
        P(None, "tile"),
        P("tile", None),
        P(),
    )
    return jax.shard_map(
        functools.partial(shards, mesh.shape["tile"], mesh.shape["blk"]),
        mesh=mesh,
        in_specs=placed,
        out_specs=P(("blk", "tile"), None),
        check_vma=False,
    )
```

```python
import functools
import math

import jax
import jax.numpy as jnp
from jax import lax
from jax.experimental import pallas as pl
from jax.experimental.pallas import tpu as pltpu
from jax.sharding import PartitionSpec as P

SIDE = 8
HD = 96
THIRD = HD // 3
LANES = 128
F32 = jnp.float32
BF16 = jnp.bfloat16
GROUP = 16
PART = 8


def dot(a, b):
    return jnp.dot(a, b, preferred_element_type=F32)


def neighbours(rows):
    col = lax.broadcasted_iota(jnp.int32, rows.shape, 1)
    left = jnp.where(col >= 1, pltpu.roll(rows, 1, axis=1), 0.0)
    right = jnp.where(col <= SIDE - 2, pltpu.roll(rows, SIDE - 1, axis=1), 0.0)
    return left, rows, right


def row_combinations(d):
    even, odd = d[4] - 4.0 * d[2], d[3] - 4.0 * d[1]
    even2, odd2 = d[4] - d[2], 2.0 * (d[3] - d[1])
    return (
        d[0] - 1.25 * d[2] + 0.25 * d[4],
        even + odd,
        even - odd,
        even2 + odd2,
        even2 - odd2,
        4.0 * d[1] - 5.0 * d[3] + d[5],
    )


def tap_combinations(g):
    near, far = g[0] + g[2], g[0] + g[2] * 4
    double = g[1] * 2
    return near + g[1], near - g[1], far + double, far - double


def four_rows(m):
    near, near_odd = (m[1] + m[2]) * (-1 / 6), (m[1] - m[2]) * (-1 / 6)
    far, far_odd = (m[3] + m[4]) * (1 / 24), (m[3] - m[4]) * (1 / 24)
    return (
        m[0] + near + far,
        near_odd + 2.0 * far_odd,
        near + 4.0 * far,
        near_odd + 8.0 * far_odd + m[5],
    )


def encode_kernel(
    x_hbm, wr_hbm, ws_hbm, we_hbm, wm_hbm, emb,
    x, wr, ws, we, mixed_taps, reduced, products, pooled, x_sems, tap_sems, sems,
):
    step = pl.program_id(0)
    count, c = pooled.shape
    area = SIDE * SIDE
    mid = wr.shape[1]
    groups = count // GROUP
    per = GROUP // PART
    parts = groups * per
    early = 2 * per
    chunk = 3 * mid // early
    last = 2 * groups - 1

    def x_copy(g):
        at = pl.ds(pl.multiple_of(g * PART * area, PART * area), PART * area)
        return pltpu.make_async_copy(x_hbm.at[at], x.at[at], x_sems.at[g])

    def tap_copy(g):
        at = pl.ds(pl.multiple_of(g * chunk, chunk), chunk)
        return pltpu.make_async_copy(ws_hbm.at[:, at], ws.at[:, at], tap_sems.at[g])

    wm = x.at[: wm_hbm.shape[0], : wm_hbm.shape[1]]
    wr_copy, we_copy, wm_copy = (
        pltpu.make_async_copy(src, dst, sems.at[i])
        for i, (src, dst) in enumerate(((wr_hbm, wr), (we_hbm, we), (wm_hbm, wm)))
    )

    @pl.when(step == 0)
    def _():
        x_copy(0).start()
        wr_copy.start()
        x_copy(1).start()
        tap_copy(0).start()
        wr_copy.wait()

    @pl.when((step == 0) | ((lax.rem(step, 2) == 1) & (step < last)))
    def _():
        @pl.loop(0, per)
        def _(i):
            g = (step + 1) // 2 * per + i
            x_copy(g).wait()

            @pl.when(g + 2 < parts)
            def _():
                x_copy(g + 2).start()

            @pl.when(g + 1 < early)
            def _():
                tap_copy(g + 1).start()

            @pl.when(g == early - 1)
            def _():
                we_copy.start()

            rows = x[pl.ds(pl.multiple_of(g * PART * area, PART * area), PART * area), :]
            maps = jnp.maximum(dot(rows, wr[...]), 0.0).reshape(PART, SIDE, SIDE, mid)
            reduced[:, pl.ds(pl.multiple_of(g * PART, PART), PART)] = maps.swapaxes(0, 1)

            @pl.when(g < early)
            def _():
                tap_copy(g).wait()
                at = pl.ds(pl.multiple_of(g * chunk, chunk), chunk)
                for k, taps in enumerate(tap_combinations([ws[dy, at, :] for dy in range(3)])):
                    mixed_taps[k, at, :] = taps

    @pl.when(step == 2)
    def _():
        we_copy.wait()

    @pl.when(step == last)
    def _():
        wm_copy.start()

    @pl.when(((lax.rem(step, 2) == 0) & (step > 0)) | (step == last))
    def _():
        g = jnp.where(step == last, groups - 1, step // 2 - 1)
        band = GROUP * SIDE
        maps = reduced[:, pl.ds(pl.multiple_of(g * GROUP, GROUP), GROUP)].reshape(SIDE, band, mid)
        edge = jnp.zeros((band, mid), F32)
        d = [edge] + [maps[i] for i in range(SIDE)] + [edge]
        upper, lower = row_combinations(d[0:6]), row_combinations(d[4:10])
        taps = [ws.at[0]] + [mixed_taps.at[k] for k in range(4)] + [ws.at[2]]
        for k in range(6):
            both = jnp.concatenate([upper[k], lower[k]], axis=0).reshape(2 * GROUP, SIDE, mid)
            window = [p.reshape(2 * band, mid).astype(BF16) for p in neighbours(both)]
            products[k] = dot(jnp.concatenate(window, axis=1), taps[k][...])
        rows = four_rows([products[k, :band] for k in range(6)])
        rows += four_rows([products[k, band:] for k in range(6)])
        spatial = jnp.stack([jnp.maximum(r, 0.0).reshape(GROUP, SIDE, mid) for r in rows], axis=0)
        spatial = spatial.swapaxes(0, 1).reshape(GROUP * area, mid).astype(BF16)
        at = pl.ds(pl.multiple_of(g * GROUP * area, GROUP * area), GROUP * area)
        out = jnp.maximum(dot(spatial, we[...]) + x[at, :].astype(F32), 0.0)
        mean = jnp.sum(out.reshape(GROUP, area, c), axis=1) * (1.0 / area)
        pooled[pl.ds(pl.multiple_of(g * GROUP, GROUP), GROUP), :] = mean

    @pl.when(step == last)
    def _():
        wm_copy.wait()
        emb[...] = dot(pooled[...].astype(BF16), wm[...]).astype(BF16)


def encode(flat, wr, ws, we, wm):
    total, c = flat.shape
    count = total // (SIDE * SIDE)
    assert wm.shape[0] <= total - GROUP * SIDE * SIDE and wm.shape[1] <= c
    mid = wr.shape[1]
    return pl.pallas_call(
        encode_kernel,
        grid=(2 * count // GROUP,),
        in_specs=[pl.BlockSpec(memory_space=pl.ANY)] * 5,
        out_specs=pl.BlockSpec((count, wm.shape[1]), lambda i: (0, 0)),
        out_shape=jax.ShapeDtypeStruct((count, wm.shape[1]), BF16),
        scratch_shapes=[
            pltpu.VMEM(flat.shape, BF16),
            pltpu.VMEM(wr.shape, BF16),
            pltpu.VMEM(ws.shape, BF16),
            pltpu.VMEM(we.shape, BF16),
            pltpu.VMEM((4,) + ws.shape[1:], BF16),
            pltpu.VMEM((SIDE, count, SIDE, mid), F32),
            pltpu.VMEM((6, 2 * GROUP * SIDE, mid), F32),
            pltpu.VMEM((count, c), F32),
            pltpu.SemaphoreType.DMA((count // PART,)),
            pltpu.SemaphoreType.DMA((2 * GROUP // PART,)),
            pltpu.SemaphoreType.DMA((3,)),
        ],
        compiler_params=pltpu.CompilerParams(vmem_limit_bytes=54 << 20),
        cost_estimate=pl.CostEstimate(
            flops=2 * total * (2 * c * mid + 9 * mid**2),
            bytes_accessed=2 * (total * c + wr.size + ws.size + we.size + wm.size),
            transcendentals=0,
        ),
        name="encode",
    )(flat, wr, ws, we, wm)


def project_kernel(heads, spread_of, emb, wq, wk, wv, *outs):
    a = lax.axis_index("blk") // spread_of
    scratch = outs[-1]
    rows = emb.shape[0]
    values = emb[...].astype(F32)
    center = jnp.mean(values, axis=1, keepdims=True)
    values = values - center
    spread = jnp.mean(values * values, axis=1, keepdims=True)
    normed = (values * lax.rsqrt(spread + 1e-05)).astype(BF16)
    query, key, value = (dot(normed, w[...]) for w in (wq, wk, wv))
    for head in range(heads):
        q, k, v = (r[:, head * HD : (head + 1) * HD] for r in (query, key, value))
        first = jnp.concatenate([q, v[:, 2 * THIRD :]], axis=1)
        second = jnp.concatenate([k, v[:, THIRD : 2 * THIRD]], axis=1)
        quarter = rows // 4
        third = jnp.concatenate([v[i * quarter : (i + 1) * quarter, :THIRD] for i in range(4)], axis=1)
        scratch[head] = jnp.concatenate([first, second, third], axis=0).astype(BF16)
    for e in range(heads):
        outs[e][...] = scratch[a ^ e]


def project(emb, wq, wk, wv, heads, spread_of):
    rows = emb.shape[0]
    packed = 2 * rows + rows // 4
    return pl.pallas_call(
        functools.partial(project_kernel, heads, spread_of),
        out_shape=[jax.ShapeDtypeStruct((packed, LANES), BF16)] * heads,
        scratch_shapes=[pltpu.VMEM((heads, packed, LANES), BF16)],
        compiler_params=pltpu.CompilerParams(vmem_limit_bytes=24 << 20),
        name="project",
    )(emb, wq, wk, wv)


def unpack_kernel(heads, *refs):
    own, query, key_value = refs[:heads], refs[heads], refs[heads + 1]
    rows = own[0].shape[0] * 4 // 9
    lane = lax.broadcasted_iota(jnp.int32, (rows, LANES), 1)
    for e in range(heads):
        first = own[e][:rows].astype(F32)
        second = own[e][rows : 2 * rows].astype(F32)
        third = own[e][2 * rows :].astype(F32)
        low = jnp.concatenate(
            [third] + [pltpu.roll(third, LANES - i * THIRD, axis=1) for i in range(1, 4)], axis=0
        )
        middle = pltpu.roll(second, 2 * THIRD, axis=1)
        high = pltpu.roll(first, 3 * THIRD, axis=1)
        value = jnp.where(lane < THIRD, low, jnp.where(lane < 2 * THIRD, middle, high))
        value = jnp.where(lane < HD, value, jnp.where(lane == HD, 1.0, 0.0))
        key = jnp.where(lane < HD, second, 0.0)
        query[e * rows : (e + 1) * rows] = own[e][:rows]
        key_value[e * rows : (e + 1) * rows, :LANES] = key.astype(BF16)
        key_value[e * rows : (e + 1) * rows, LANES:] = value.astype(BF16)


def unpack(own):
    heads, rows = len(own), own[0].shape[0] * 4 // 9
    return pl.pallas_call(
        functools.partial(unpack_kernel, heads),
        out_shape=[
            jax.ShapeDtypeStruct((heads * rows, LANES), BF16),
            jax.ShapeDtypeStruct((heads * rows, 2 * LANES), BF16),
        ],
        compiler_params=pltpu.CompilerParams(vmem_limit_bytes=24 << 20),
        name="unpack",
    )(*own)


class Slides:
    def __init__(self, slide_tiles, heads, spread_of, length):
        blk = lax.axis_index("blk")
        self.a, self.c = blk // spread_of, lax.rem(blk, spread_of)
        self.heads, self.spread_of, self.length = heads, spread_of, length
        first = slide_tiles[0]
        second = first + slide_tiles[1]
        self.ends = (first, second, second + slide_tiles[2])

    def of(self, e, f, dim):
        shape = (self.length, 1) if dim == 0 else (1, self.length)
        start = ((self.a ^ e) * self.spread_of + (self.c ^ f)) * self.length
        pos = lax.broadcasted_iota(jnp.int32, shape, dim) + start
        return sum((pos >= end).astype(jnp.int32) for end in self.ends)

    def of_rows(self):
        return jnp.concatenate([self.of(e, 0, 0) for e in range(self.heads)], axis=0)

    def of_keys(self, f):
        return jnp.concatenate([self.of(e, f, 1) for e in range(self.heads)], axis=1)


SCALE = math.log2(math.e) / math.sqrt(HD)


def masked_scores(query, keys, query_slide, key_slide):
    scores = lax.dot_general(query, keys, (((1,), (1,)), ((), ())), preferred_element_type=F32)
    return jnp.where(query_slide == key_slide, scores, -1e30)


def attend_own_kernel(heads, spread_of, slide_tiles, queries, key_value, out):
    rows = queries.shape[0]
    slides = Slides(slide_tiles, heads, spread_of, rows // heads)
    lane = lax.broadcasted_iota(jnp.int32, (rows, LANES), 1)
    scores = masked_scores(queries[...], key_value[:, :LANES], slides.of_rows(), slides.of_keys(0))
    top = jnp.max(scores, axis=1, keepdims=True)
    product = dot(jnp.exp2((scores - top) * SCALE).astype(BF16), key_value[:, LANES:])
    out[...] = jnp.where(lane == HD + 1, top, product)


def attend_others_kernel(heads, spread_of, slide_tiles, queries, before, *refs):
    others, outs = refs[: spread_of - 1], refs[spread_of - 1 :]
    length = queries.shape[0] // heads
    slides = Slides(slide_tiles, heads, spread_of, length)
    query_slide = slides.of_rows()
    quarter = length // 4
    scores = [
        masked_scores(queries[...], other[:, :LANES], query_slide, slides.of_keys(f))
        for f, other in enumerate(others, start=1)
    ]
    top_before = before[:, HD + 1 : HD + 2]
    top = functools.reduce(jnp.maximum, [jnp.max(s, axis=1, keepdims=True) for s in scores], top_before)
    product = before[...] * jnp.exp2((top_before - top) * SCALE)
    for other, s in zip(others, scores):
        product = product + dot(jnp.exp2((s - top) * SCALE).astype(BF16), other[:, LANES:])
    result = product[:, :HD] / product[:, HD : HD + 1]
    for e in range(heads):
        head = result[e * length : e * length + 3 * quarter]
        rest = result[e * length + 3 * quarter : (e + 1) * length]
        rest = jnp.concatenate([rest[:, i * THIRD : (i + 1) * THIRD] for i in range(3)], axis=0)
        outs[e][...] = jnp.concatenate([head, rest], axis=1).astype(BF16)


def attend(slide_tiles, own, exchange):
    queries, key_value = unpack(own)
    heads, rows = len(own), queries.shape[0]
    length = rows // heads
    others = exchange(key_value)
    spread_of = len(others) + 1
    small = pl.BlockSpec(memory_space=pltpu.SMEM)
    whole = pl.BlockSpec(memory_space=pltpu.VMEM)
    params = pltpu.CompilerParams(vmem_limit_bytes=40 << 20)
    cost = pl.CostEstimate(
        flops=4 * rows * rows * LANES, bytes_accessed=6 * rows * LANES, transcendentals=rows * rows
    )
    partial = pl.pallas_call(
        functools.partial(attend_own_kernel, heads, spread_of),
        in_specs=[small] + [whole] * 2,
        out_specs=whole,
        out_shape=jax.ShapeDtypeStruct((rows, LANES), F32),
        compiler_params=params,
        cost_estimate=cost,
        name="attend_own",
    )(slide_tiles, queries, key_value)
    packed = (length * 3 // 4, LANES)
    return pl.pallas_call(
        functools.partial(attend_others_kernel, heads, spread_of),
        in_specs=[small] + [whole] * (1 + spread_of),
        out_specs=[whole] * heads,
        out_shape=[jax.ShapeDtypeStruct(packed, BF16)] * heads,
        compiler_params=params,
        name="attend_others",
    )(slide_tiles, queries, partial, *others)


def partial_out_kernel(heads, tiles_of, spread_of, *refs):
    parts, w_out, outs = refs[:heads], refs[heads], refs[heads + 1 : heads + 1 + tiles_of]
    sorted_heads, sums = refs[heads + 1 + tiles_of :]
    a, t = lax.axis_index("blk") // spread_of, lax.axis_index("tile")
    quarter = parts[0].shape[0] // 3
    for e in range(heads):
        packed = parts[e][...].astype(F32)
        tail = packed[:, HD:]
        rest = jnp.concatenate([tail[i * quarter : (i + 1) * quarter] for i in range(3)], axis=1)
        sorted_heads[a ^ e] = jnp.concatenate([packed[:, :HD], rest], axis=0)
    attended = jnp.concatenate([sorted_heads[h] for h in range(heads)], axis=1).astype(BF16)
    product = dot(attended, w_out[...])
    count = product.shape[0] // tiles_of
    for block in range(tiles_of):
        sums[block] = product[block * count : (block + 1) * count]
    for d in range(tiles_of):
        outs[d][...] = sums[t ^ d].astype(outs[d].dtype)


def partial_out(parts, w_out, tiles_of, spread_of):
    heads, width = len(parts), w_out.shape[1]
    length = parts[0].shape[0] * 4 // 3
    count = length // tiles_of
    whole = pl.BlockSpec(memory_space=pltpu.VMEM)
    return pl.pallas_call(
        functools.partial(partial_out_kernel, heads, tiles_of, spread_of),
        in_specs=[whole] * (heads + 1),
        out_specs=[whole] * tiles_of,
        out_shape=[jax.ShapeDtypeStruct((count, width), F32 if d == 0 else BF16) for d in range(tiles_of)],
        scratch_shapes=[pltpu.VMEM((heads, length, HD), F32), pltpu.VMEM((tiles_of, count, width), F32)],
        compiler_params=pltpu.CompilerParams(vmem_limit_bytes=24 << 20),
        name="partial_out",
    )(*parts, w_out)


def finish_kernel(emb, *refs):
    total = emb[...].astype(F32)
    for ref in refs[:-1]:
        total = total + ref[...].astype(F32)
    refs[-1][...] = total.astype(BF16)


def finish(emb, sums):
    return pl.pallas_call(
        finish_kernel,
        out_shape=jax.ShapeDtypeStruct(emb.shape, BF16),
        compiler_params=pltpu.CompilerParams(vmem_limit_bytes=24 << 20),
        name="finish",
    )(emb, *sums)


def shards(tiles_of, blks, tiles, wr, ws, we, wm, wq, wk, wv, wo, slide_tiles):
    count = tiles.shape[0]
    flat = tiles.reshape(count * SIDE * SIDE, tiles.shape[3])
    mid = wr.shape[1]
    heads = wq.shape[1] // HD
    spread_of = blks // heads

    def along(x, axis, size, step):
        return lax.ppermute(x, axis, [(i, i ^ step) for i in range(size)])

    def over_heads(blocks):
        return [blocks[0]] + [along(blocks[e], "blk", blks, e * spread_of) for e in range(1, heads)]

    emb = encode(flat, wr, ws.reshape(3, 3 * mid, mid), we, wm)
    gathered = lax.all_gather(emb, "tile", axis=0, tiled=True)
    own = over_heads(project(gathered, wq, wk, wv, heads, spread_of))
    attended = attend(
        slide_tiles, own, lambda x: [along(x, "blk", blks, f) for f in range(1, spread_of)]
    )
    sums = partial_out(over_heads(attended), wo, tiles_of, spread_of)
    sums = [sums[0]] + [along(sums[d], "tile", tiles_of, d) for d in range(1, tiles_of)]
    return finish(emb, sums)


def solution(mesh):
    placed = (
        P(("blk", "tile"), None, None, None),
        P(),
        P(),
        P(),
        P(),
        P(None, "tile"),
        P(None, "tile"),
        P(None, "tile"),
        P("tile", None),
        P(),
    )
    return jax.shard_map(
        functools.partial(shards, mesh.shape["tile"], mesh.shape["blk"]),
        mesh=mesh,
        in_specs=placed,
        out_specs=P(("blk", "tile"), None),
        check_vma=False,
    )
```

```python
import functools
import math

import jax
import jax.numpy as jnp
from jax import lax
from jax.experimental import pallas as pl
from jax.experimental.pallas import tpu as pltpu
from jax.sharding import PartitionSpec as P

SIDE = 8
HD = 96
THIRD = HD // 3
LANES = 128
F32 = jnp.float32
BF16 = jnp.bfloat16
GROUP = 16
PART = 8


def dot(a, b):
    return jnp.dot(a, b, preferred_element_type=F32)


def neighbours(rows):
    col = lax.broadcasted_iota(jnp.int32, rows.shape, 1)
    left = jnp.where(col >= 1, pltpu.roll(rows, 1, axis=1), 0.0)
    right = jnp.where(col <= SIDE - 2, pltpu.roll(rows, SIDE - 1, axis=1), 0.0)
    return left, rows, right


def row_combinations(d):
    even, odd = d[4] - 4.0 * d[2], d[3] - 4.0 * d[1]
    even2, odd2 = d[4] - d[2], 2.0 * (d[3] - d[1])
    return (
        d[0] - 1.25 * d[2] + 0.25 * d[4],
        even + odd,
        even - odd,
        even2 + odd2,
        even2 - odd2,
        4.0 * d[1] - 5.0 * d[3] + d[5],
    )


def tap_combinations(g):
    near, far = g[0] + g[2], g[0] + g[2] * 4
    double = g[1] * 2
    return near + g[1], near - g[1], far + double, far - double


def four_rows(m):
    near, near_odd = (m[1] + m[2]) * (-1 / 6), (m[1] - m[2]) * (-1 / 6)
    far, far_odd = (m[3] + m[4]) * (1 / 24), (m[3] - m[4]) * (1 / 24)
    return (
        m[0] + near + far,
        near_odd + 2.0 * far_odd,
        near + 4.0 * far,
        near_odd + 8.0 * far_odd + m[5],
    )


def encode_kernel(
    x_hbm, wr_hbm, ws_hbm, we_hbm, wm_hbm, emb,
    x, wr, ws, we, mixed_taps, reduced, products, pooled, x_sems, tap_sems, sems,
):
    step = pl.program_id(0)
    count, c = pooled.shape
    area = SIDE * SIDE
    mid = wr.shape[1]
    groups = count // GROUP
    per = GROUP // PART
    parts = groups * per
    early = 2 * per
    chunk = 3 * mid // early
    last = 2 * groups - 1

    def x_copy(g):
        at = pl.ds(pl.multiple_of(g * PART * area, PART * area), PART * area)
        return pltpu.make_async_copy(x_hbm.at[at], x.at[at], x_sems.at[g])

    def tap_copy(g):
        at = pl.ds(pl.multiple_of(g * chunk, chunk), chunk)
        return pltpu.make_async_copy(ws_hbm.at[:, at], ws.at[:, at], tap_sems.at[g])

    wm = x.at[: wm_hbm.shape[0], : wm_hbm.shape[1]]
    wr_copy, we_copy, wm_copy = (
        pltpu.make_async_copy(src, dst, sems.at[i])
        for i, (src, dst) in enumerate(((wr_hbm, wr), (we_hbm, we), (wm_hbm, wm)))
    )

    @pl.when(step == 0)
    def _():
        x_copy(0).start()
        wr_copy.start()
        x_copy(1).start()
        tap_copy(0).start()
        wr_copy.wait()

    @pl.when((step == 0) | ((lax.rem(step, 2) == 1) & (step < last)))
    def _():
        @pl.loop(0, per)
        def _(i):
            g = (step + 1) // 2 * per + i
            x_copy(g).wait()

            @pl.when(g + 2 < parts)
            def _():
                x_copy(g + 2).start()

            @pl.when(g + 1 < early)
            def _():
                tap_copy(g + 1).start()

            @pl.when(g == early - 1)
            def _():
                we_copy.start()

            rows = x[pl.ds(pl.multiple_of(g * PART * area, PART * area), PART * area), :]
            maps = jnp.maximum(dot(rows, wr[...]), 0.0).reshape(PART, SIDE, SIDE, mid)
            reduced[:, pl.ds(pl.multiple_of(g * PART, PART), PART)] = maps.swapaxes(0, 1)

            @pl.when(g < early)
            def _():
                tap_copy(g).wait()
                at = pl.ds(pl.multiple_of(g * chunk, chunk), chunk)
                for k, taps in enumerate(tap_combinations([ws[dy, at, :] for dy in range(3)])):
                    mixed_taps[k, at, :] = taps

    @pl.when(step == 2)
    def _():
        we_copy.wait()

    @pl.when(step == last)
    def _():
        wm_copy.start()

    @pl.when(((lax.rem(step, 2) == 0) & (step > 0)) | (step == last))
    def _():
        g = jnp.where(step == last, groups - 1, step // 2 - 1)
        band = GROUP * SIDE
        maps = reduced[:, pl.ds(pl.multiple_of(g * GROUP, GROUP), GROUP)].reshape(SIDE, band, mid)
        edge = jnp.zeros((band, mid), F32)
        d = [edge] + [maps[i] for i in range(SIDE)] + [edge]
        upper, lower = row_combinations(d[0:6]), row_combinations(d[4:10])
        taps = [ws.at[0]] + [mixed_taps.at[k] for k in range(4)] + [ws.at[2]]
        for k in range(6):
            both = jnp.concatenate([upper[k], lower[k]], axis=0).reshape(2 * GROUP, SIDE, mid)
            window = [p.reshape(2 * band, mid).astype(BF16) for p in neighbours(both)]
            products[k] = dot(jnp.concatenate(window, axis=1), taps[k][...])
        rows = four_rows([products[k, :band] for k in range(6)])
        rows += four_rows([products[k, band:] for k in range(6)])
        spatial = jnp.stack([jnp.maximum(r, 0.0).reshape(GROUP, SIDE, mid) for r in rows], axis=0)
        spatial = spatial.swapaxes(0, 1).reshape(GROUP * area, mid).astype(BF16)
        at = pl.ds(pl.multiple_of(g * GROUP * area, GROUP * area), GROUP * area)
        out = jnp.maximum(dot(spatial, we[...]) + x[at, :].astype(F32), 0.0)
        mean = jnp.sum(out.reshape(GROUP, area, c), axis=1) * (1.0 / area)
        pooled[pl.ds(pl.multiple_of(g * GROUP, GROUP), GROUP), :] = mean

    @pl.when(step == last)
    def _():
        wm_copy.wait()
        emb[...] = dot(pooled[...].astype(BF16), wm[...]).astype(BF16)


def encode(flat, wr, ws, we, wm):
    total, c = flat.shape
    count = total // (SIDE * SIDE)
    assert wm.shape[0] <= total - GROUP * SIDE * SIDE and wm.shape[1] <= c
    mid = wr.shape[1]
    return pl.pallas_call(
        encode_kernel,
        grid=(2 * count // GROUP,),
        in_specs=[pl.BlockSpec(memory_space=pl.ANY)] * 5,
        out_specs=pl.BlockSpec((count, wm.shape[1]), lambda i: (0, 0)),
        out_shape=jax.ShapeDtypeStruct((count, wm.shape[1]), BF16),
        scratch_shapes=[
            pltpu.VMEM(flat.shape, BF16),
            pltpu.VMEM(wr.shape, BF16),
            pltpu.VMEM(ws.shape, BF16),
            pltpu.VMEM(we.shape, BF16),
            pltpu.VMEM((4,) + ws.shape[1:], BF16),
            pltpu.VMEM((SIDE, count, SIDE, mid), F32),
            pltpu.VMEM((6, 2 * GROUP * SIDE, mid), F32),
            pltpu.VMEM((count, c), F32),
            pltpu.SemaphoreType.DMA((count // PART,)),
            pltpu.SemaphoreType.DMA((2 * GROUP // PART,)),
            pltpu.SemaphoreType.DMA((3,)),
        ],
        compiler_params=pltpu.CompilerParams(vmem_limit_bytes=52 << 20),
        cost_estimate=pl.CostEstimate(
            flops=2 * total * (2 * c * mid + 9 * mid**2),
            bytes_accessed=2 * (total * c + wr.size + ws.size + we.size + wm.size),
            transcendentals=0,
        ),
        name="encode",
    )(flat, wr, ws, we, wm)


def project_kernel(heads, spread_of, blocks, *refs):
    embs, (wq, wk, wv) = refs[:blocks], refs[blocks : blocks + 3]
    outs, scratch = refs[blocks + 3 : -1], refs[-1]
    a = lax.axis_index("blk") // spread_of
    values = jnp.concatenate([emb[...].astype(F32) for emb in embs], axis=0)
    rows = values.shape[0]
    center = jnp.mean(values, axis=1, keepdims=True)
    values = values - center
    spread = jnp.mean(values * values, axis=1, keepdims=True)
    normed = (values * lax.rsqrt(spread + 1e-05)).astype(BF16)
    query, key, value = (dot(normed, w[...]) for w in (wq, wk, wv))
    for head in range(heads):
        q, k, v = (r[:, head * HD : (head + 1) * HD] for r in (query, key, value))
        first = jnp.concatenate([q, v[:, 2 * THIRD :]], axis=1)
        second = jnp.concatenate([k, v[:, THIRD : 2 * THIRD]], axis=1)
        quarter = rows // 4
        third = jnp.concatenate([v[i * quarter : (i + 1) * quarter, :THIRD] for i in range(4)], axis=1)
        scratch[head] = jnp.concatenate([first, second, third], axis=0).astype(BF16)
    for e in range(heads):
        outs[e][...] = scratch[a ^ e]


def project(embs, wq, wk, wv, heads, spread_of):
    rows = embs[0].shape[0] * len(embs)
    packed = 2 * rows + rows // 4
    whole = pl.BlockSpec(memory_space=pltpu.VMEM)
    return pl.pallas_call(
        functools.partial(project_kernel, heads, spread_of, len(embs)),
        in_specs=[whole] * (len(embs) + 3),
        out_specs=[whole] * heads,
        out_shape=[jax.ShapeDtypeStruct((packed, LANES), BF16)] * heads,
        scratch_shapes=[pltpu.VMEM((heads, packed, LANES), BF16)],
        compiler_params=pltpu.CompilerParams(vmem_limit_bytes=24 << 20),
        cost_estimate=pl.CostEstimate(
            flops=6 * rows * wq.size, bytes_accessed=6 * wq.size, transcendentals=0
        ),
        name="project",
    )(*embs, wq, wk, wv)


def unpack_kernel(packs, *refs):
    query, key_value = refs[packs:]
    at = 0
    for pack in refs[:packs]:
        rows = pack.shape[0] * 4 // 9
        lane = lax.broadcasted_iota(jnp.int32, (rows, LANES), 1)
        first = pack[:rows].astype(F32)
        second = pack[rows : 2 * rows].astype(F32)
        third = pack[2 * rows :].astype(F32)
        low = jnp.concatenate(
            [third] + [pltpu.roll(third, LANES - i * THIRD, axis=1) for i in range(1, 4)], axis=0
        )
        middle = pltpu.roll(second, 2 * THIRD, axis=1)
        high = pltpu.roll(first, 3 * THIRD, axis=1)
        value = jnp.where(lane < THIRD, low, jnp.where(lane < 2 * THIRD, middle, high))
        value = jnp.where(lane < HD, value, jnp.where(lane == HD, 1.0, 0.0))
        key = jnp.where(lane < HD, second, 0.0)
        query[at : at + rows] = pack[:rows]
        key_value[at : at + rows, :LANES] = key.astype(BF16)
        key_value[at : at + rows, LANES:] = value.astype(BF16)
        at += rows


def unpack(packs):
    rows = sum(pack.shape[0] * 4 // 9 for pack in packs)
    whole = pl.BlockSpec(memory_space=pltpu.VMEM)
    return pl.pallas_call(
        functools.partial(unpack_kernel, len(packs)),
        in_specs=[whole] * len(packs),
        out_specs=[whole] * 2,
        out_shape=[
            jax.ShapeDtypeStruct((rows, LANES), BF16),
            jax.ShapeDtypeStruct((rows, 2 * LANES), BF16),
        ],
        compiler_params=pltpu.CompilerParams(vmem_limit_bytes=24 << 20),
        name="unpack",
    )(*packs)


class Layout:
    def __init__(self, slide_tiles, heads, spread_of, sets, count):
        blk = lax.axis_index("blk")
        self.t, self.a, self.c = lax.axis_index("tile"), blk // spread_of, lax.rem(blk, spread_of)
        self.spread_of, self.count = spread_of, count
        self.tiles_of = sum(len(members) for members in sets)
        self.blocks = [(e, d) for members in sets for e in range(heads) for d in members]
        first = slide_tiles[0]
        second = first + slide_tiles[1]
        self.ends = (first, second, second + slide_tiles[2])

    def starts(self, f):
        shards = [((self.a ^ e) * self.spread_of + (self.c ^ f), self.t ^ d) for e, d in self.blocks]
        return [(shard * self.tiles_of + tile) * self.count for shard, tile in shards]

    def slide_of(self, positions):
        return sum((positions >= end).astype(jnp.int32) for end in self.ends)

    def of_rows(self):
        row = lax.broadcasted_iota(jnp.int32, (self.count, 1), 0)
        return jnp.concatenate([self.slide_of(row + start) for start in self.starts(0)], axis=0)

    def of_keys(self, f):
        lane = lax.broadcasted_iota(jnp.int32, (1, len(self.blocks) * self.count), 1)
        starts = self.starts(f)
        positions = lane + starts[0]
        for i in range(1, len(starts)):
            step = starts[i] - starts[i - 1] - self.count
            positions = positions + jnp.where(lane >= i * self.count, step, 0)
        return self.slide_of(positions)


SCALE = math.log2(math.e) / math.sqrt(HD)


def masked_scores(query, keys, query_slide, key_slide):
    scores = lax.dot_general(query, keys, (((1,), (1,)), ((), ())), preferred_element_type=F32)
    return jnp.where(query_slide == key_slide, scores, -1e30)


def attend_own_kernel(layout, slide_tiles, queries, key_value, out):
    rows = layout(slide_tiles)
    lane = lax.broadcasted_iota(jnp.int32, out.shape, 1)
    scores = masked_scores(queries[...], key_value[:, :LANES], rows.of_rows(), rows.of_keys(0))
    top = jnp.max(scores, axis=1, keepdims=True)
    product = dot(jnp.exp2((scores - top) * SCALE).astype(BF16), key_value[:, LANES:])
    out[...] = jnp.where(lane == HD + 1, top, product)


def attend_others_kernel(layout, others_count, slide_tiles, queries, before, *refs):
    others, outs = refs[:others_count], refs[others_count:]
    rows = layout(slide_tiles)
    query_slide = rows.of_rows()
    scores = [
        masked_scores(queries[...], other[:, :LANES], query_slide, rows.of_keys(f))
        for f, other in enumerate(others, start=1)
    ]
    top_before = before[:, HD + 1 : HD + 2]
    top = functools.reduce(jnp.maximum, [jnp.max(s, axis=1, keepdims=True) for s in scores], top_before)
    product = before[...] * jnp.exp2((top_before - top) * SCALE)
    for other, s in zip(others, scores):
        product = product + dot(jnp.exp2((s - top) * SCALE).astype(BF16), other[:, LANES:])
    result = product[:, :HD] / product[:, HD : HD + 1]
    count = rows.count
    quarter = rows.tiles_of * count // 4
    for e in range(len(outs)):
        places = [rows.blocks.index((e, d)) * count for d in range(rows.tiles_of)]
        here = jnp.concatenate([result[at : at + count] for at in places], axis=0)
        rest = here[3 * quarter :]
        rest = jnp.concatenate([rest[:, i * THIRD : (i + 1) * THIRD] for i in range(3)], axis=0)
        outs[e][...] = jnp.concatenate([here[: 3 * quarter], rest], axis=1).astype(BF16)


def attend(slide_tiles, packs, heads, sets, count, exchange):
    queries, key_value = unpack(packs)
    rows = queries.shape[0]
    others = exchange(key_value)
    spread_of = len(others) + 1

    def layout(slide_tiles):
        return Layout(slide_tiles, heads, spread_of, sets, count)

    small = pl.BlockSpec(memory_space=pltpu.SMEM)
    whole = pl.BlockSpec(memory_space=pltpu.VMEM)
    params = pltpu.CompilerParams(vmem_limit_bytes=40 << 20)
    cost = pl.CostEstimate(
        flops=4 * rows * rows * LANES, bytes_accessed=6 * rows * LANES, transcendentals=rows * rows
    )
    partial = pl.pallas_call(
        functools.partial(attend_own_kernel, layout),
        in_specs=[small] + [whole] * 2,
        out_specs=whole,
        out_shape=jax.ShapeDtypeStruct((rows, LANES), F32),
        compiler_params=params,
        cost_estimate=cost,
        name="attend_own",
    )(slide_tiles, queries, key_value)
    packed = (rows // heads * 3 // 4, LANES)
    return pl.pallas_call(
        functools.partial(attend_others_kernel, layout, len(others)),
        in_specs=[small] + [whole] * (1 + spread_of),
        out_specs=[whole] * heads,
        out_shape=[jax.ShapeDtypeStruct(packed, BF16)] * heads,
        compiler_params=params,
        name="attend_others",
    )(slide_tiles, queries, partial, *others)


def partial_out_kernel(heads, tiles_of, spread_of, *refs):
    parts, w_out, outs = refs[:heads], refs[heads], refs[heads + 1 : heads + 1 + tiles_of]
    sorted_heads = refs[-1]
    a = lax.axis_index("blk") // spread_of
    quarter = parts[0].shape[0] // 3
    for e in range(heads):
        packed = parts[e][...].astype(F32)
        tail = packed[:, HD:]
        rest = jnp.concatenate([tail[i * quarter : (i + 1) * quarter] for i in range(3)], axis=1)
        sorted_heads[a ^ e] = jnp.concatenate([packed[:, :HD], rest], axis=0)
    attended = jnp.concatenate([sorted_heads[h] for h in range(heads)], axis=1).astype(BF16)
    product = dot(attended, w_out[...])
    count = product.shape[0] // tiles_of
    for d in range(tiles_of):
        outs[d][...] = product[d * count : (d + 1) * count].astype(outs[d].dtype)


def partial_out(parts, w_out, tiles_of, spread_of):
    heads, width = len(parts), w_out.shape[1]
    length = parts[0].shape[0] * 4 // 3
    count = length // tiles_of
    whole = pl.BlockSpec(memory_space=pltpu.VMEM)
    return pl.pallas_call(
        functools.partial(partial_out_kernel, heads, tiles_of, spread_of),
        in_specs=[whole] * (heads + 1),
        out_specs=[whole] * tiles_of,
        out_shape=[jax.ShapeDtypeStruct((count, width), F32 if d == 0 else BF16) for d in range(tiles_of)],
        scratch_shapes=[pltpu.VMEM((heads, length, HD), F32)],
        compiler_params=pltpu.CompilerParams(vmem_limit_bytes=24 << 20),
        name="partial_out",
    )(*parts, w_out)


def finish_kernel(emb, *refs):
    total = emb[...].astype(F32)
    for ref in refs[:-1]:
        total = total + ref[...].astype(F32)
    refs[-1][...] = total.astype(BF16)


def finish(emb, sums):
    return pl.pallas_call(
        finish_kernel,
        out_shape=jax.ShapeDtypeStruct(emb.shape, BF16),
        compiler_params=pltpu.CompilerParams(vmem_limit_bytes=24 << 20),
        name="finish",
    )(emb, *sums)


def shards(tiles_of, blks, tiles, wr, ws, we, wm, wq, wk, wv, wo, slide_tiles):
    count = tiles.shape[0]
    flat = tiles.reshape(count * SIDE * SIDE, tiles.shape[3])
    mid = wr.shape[1]
    heads = wq.shape[1] // HD
    spread_of = blks // heads

    def along(x, axis, size, step):
        return lax.ppermute(x, axis, [(i, i ^ step) for i in range(size)])

    def over_heads(blocks):
        return [blocks[0]] + [along(blocks[e], "blk", blks, e * spread_of) for e in range(1, heads)]

    emb = encode(flat, wr, ws.reshape(3, 3 * mid, mid), we, wm)
    embs = [emb] + [along(emb, "tile", tiles_of, d) for d in range(1, tiles_of)]
    sets = [range(tiles_of // 2), range(tiles_of // 2, tiles_of)]
    packs = []
    for members in sets:
        blocks = [embs[d] for d in members]
        if packs:
            *blocks, _ = lax.optimization_barrier((*blocks, packs[1]))
        packs += over_heads(project(blocks, wq, wk, wv, heads, spread_of))
    attended = attend(
        slide_tiles, packs, heads, sets, count,
        lambda x: [along(x, "blk", blks, f) for f in range(1, spread_of)],
    )
    sums = partial_out(over_heads(attended), wo, tiles_of, spread_of)
    sums = [sums[0]] + [along(sums[d], "tile", tiles_of, d) for d in range(1, tiles_of)]
    return finish(emb, sums)


def solution(mesh):
    placed = (
        P(("blk", "tile"), None, None, None),
        P(),
        P(),
        P(),
        P(),
        P(None, "tile"),
        P(None, "tile"),
        P(None, "tile"),
        P("tile", None),
        P(),
    )
    return jax.shard_map(
        functools.partial(shards, mesh.shape["tile"], mesh.shape["blk"]),
        mesh=mesh,
        in_specs=placed,
        out_specs=P(("blk", "tile"), None),
        check_vma=False,
    )
```

```python
import functools
import math

import jax
import jax.numpy as jnp
from jax import lax
from jax.experimental import pallas as pl
from jax.experimental.pallas import tpu as pltpu
from jax.sharding import PartitionSpec as P

SIDE = 8
HD = 96
THIRD = HD // 3
LANES = 128
F32 = jnp.float32
BF16 = jnp.bfloat16
GROUP = 16
PART = 8


def dot(a, b):
    return jnp.dot(a, b, preferred_element_type=F32)


def neighbours(rows):
    col = lax.broadcasted_iota(jnp.int32, rows.shape, 1)
    left = jnp.where(col >= 1, pltpu.roll(rows, 1, axis=1), 0.0)
    right = jnp.where(col <= SIDE - 2, pltpu.roll(rows, SIDE - 1, axis=1), 0.0)
    return left, rows, right


def row_combinations(d):
    even, odd = d[4] - 4.0 * d[2], d[3] - 4.0 * d[1]
    even2, odd2 = d[4] - d[2], 2.0 * (d[3] - d[1])
    return (
        d[0] - 1.25 * d[2] + 0.25 * d[4],
        even + odd,
        even - odd,
        even2 + odd2,
        even2 - odd2,
        4.0 * d[1] - 5.0 * d[3] + d[5],
    )


def tap_combinations(g):
    near, far = g[0] + g[2], g[0] + g[2] * 4
    double = g[1] * 2
    return near + g[1], near - g[1], far + double, far - double


def four_rows(m):
    near, near_odd = (m[1] + m[2]) * (-1 / 6), (m[1] - m[2]) * (-1 / 6)
    far, far_odd = (m[3] + m[4]) * (1 / 24), (m[3] - m[4]) * (1 / 24)
    return (
        m[0] + near + far,
        near_odd + 2.0 * far_odd,
        near + 4.0 * far,
        near_odd + 8.0 * far_odd + m[5],
    )


def encode_kernel(
    x_hbm, wr_hbm, ws_hbm, we_hbm, wm_hbm, emb,
    x, wr, ws, we, mixed_taps, reduced, products, pooled, x_sems, tap_sems, sems,
):
    step = pl.program_id(0)
    count, c = pooled.shape
    area = SIDE * SIDE
    mid = wr.shape[1]
    groups = count // GROUP
    per = GROUP // PART
    parts = groups * per
    early = 2 * per
    chunk = 3 * mid // early
    last = 2 * groups - 1

    def x_copy(g):
        at = pl.ds(pl.multiple_of(g * PART * area, PART * area), PART * area)
        return pltpu.make_async_copy(x_hbm.at[at], x.at[at], x_sems.at[g])

    def tap_copy(g):
        at = pl.ds(pl.multiple_of(g * chunk, chunk), chunk)
        return pltpu.make_async_copy(ws_hbm.at[:, at], ws.at[:, at], tap_sems.at[g])

    wm = x.at[: wm_hbm.shape[0], : wm_hbm.shape[1]]
    wr_copy, we_copy, wm_copy = (
        pltpu.make_async_copy(src, dst, sems.at[i])
        for i, (src, dst) in enumerate(((wr_hbm, wr), (we_hbm, we), (wm_hbm, wm)))
    )

    @pl.when(step == 0)
    def _():
        x_copy(0).start()
        wr_copy.start()
        x_copy(1).start()
        tap_copy(0).start()
        wr_copy.wait()

    @pl.when((step == 0) | ((lax.rem(step, 2) == 1) & (step < last)))
    def _():
        @pl.loop(0, per)
        def _(i):
            g = (step + 1) // 2 * per + i
            x_copy(g).wait()

            @pl.when(g + 2 < parts)
            def _():
                x_copy(g + 2).start()

            @pl.when(g + 1 < early)
            def _():
                tap_copy(g + 1).start()

            @pl.when(g == early - 1)
            def _():
                we_copy.start()

            rows = x[pl.ds(pl.multiple_of(g * PART * area, PART * area), PART * area), :]
            maps = jnp.maximum(dot(rows, wr[...]), 0.0).reshape(PART, SIDE, SIDE, mid)
            reduced[:, pl.ds(pl.multiple_of(g * PART, PART), PART)] = maps.swapaxes(0, 1)

            @pl.when(g < early)
            def _():
                tap_copy(g).wait()
                at = pl.ds(pl.multiple_of(g * chunk, chunk), chunk)
                for k, taps in enumerate(tap_combinations([ws[dy, at, :] for dy in range(3)])):
                    mixed_taps[k, at, :] = taps

    @pl.when(step == 2)
    def _():
        we_copy.wait()

    @pl.when(step == last)
    def _():
        wm_copy.start()

    @pl.when(((lax.rem(step, 2) == 0) & (step > 0)) | (step == last))
    def _():
        g = jnp.where(step == last, groups - 1, step // 2 - 1)
        band = GROUP * SIDE
        maps = reduced[:, pl.ds(pl.multiple_of(g * GROUP, GROUP), GROUP)].reshape(SIDE, band, mid)
        edge = jnp.zeros((band, mid), F32)
        d = [edge] + [maps[i] for i in range(SIDE)] + [edge]
        upper, lower = row_combinations(d[0:6]), row_combinations(d[4:10])
        taps = [ws.at[0]] + [mixed_taps.at[k] for k in range(4)] + [ws.at[2]]
        for k in range(6):
            both = jnp.concatenate([upper[k], lower[k]], axis=0).reshape(2 * GROUP, SIDE, mid)
            window = [p.reshape(2 * band, mid).astype(BF16) for p in neighbours(both)]
            products[k] = dot(jnp.concatenate(window, axis=1), taps[k][...])
        rows = four_rows([products[k, :band] for k in range(6)])
        rows += four_rows([products[k, band:] for k in range(6)])
        spatial = jnp.stack([jnp.maximum(r, 0.0).reshape(GROUP, SIDE, mid) for r in rows], axis=0)
        spatial = spatial.swapaxes(0, 1).reshape(GROUP * area, mid).astype(BF16)
        at = pl.ds(pl.multiple_of(g * GROUP * area, GROUP * area), GROUP * area)
        out = jnp.maximum(dot(spatial, we[...]) + x[at, :].astype(F32), 0.0)
        mean = jnp.sum(out.reshape(GROUP, area, c), axis=1) * (1.0 / area)
        pooled[pl.ds(pl.multiple_of(g * GROUP, GROUP), GROUP), :] = mean

    @pl.when(step == last)
    def _():
        wm_copy.wait()
        emb[...] = dot(pooled[...].astype(BF16), wm[...]).astype(BF16)


def encode(flat, wr, ws, we, wm):
    total, c = flat.shape
    count = total // (SIDE * SIDE)
    assert wm.shape[0] <= total - GROUP * SIDE * SIDE and wm.shape[1] <= c
    mid = wr.shape[1]
    return pl.pallas_call(
        encode_kernel,
        grid=(2 * count // GROUP,),
        in_specs=[pl.BlockSpec(memory_space=pl.ANY)] * 5,
        out_specs=pl.BlockSpec((count, wm.shape[1]), lambda i: (0, 0)),
        out_shape=jax.ShapeDtypeStruct((count, wm.shape[1]), BF16),
        scratch_shapes=[
            pltpu.VMEM(flat.shape, BF16),
            pltpu.VMEM(wr.shape, BF16),
            pltpu.VMEM(ws.shape, BF16),
            pltpu.VMEM(we.shape, BF16),
            pltpu.VMEM((4,) + ws.shape[1:], BF16),
            pltpu.VMEM((SIDE, count, SIDE, mid), F32),
            pltpu.VMEM((6, 2 * GROUP * SIDE, mid), F32),
            pltpu.VMEM((count, c), F32),
            pltpu.SemaphoreType.DMA((count // PART,)),
            pltpu.SemaphoreType.DMA((2 * GROUP // PART,)),
            pltpu.SemaphoreType.DMA((3,)),
        ],
        compiler_params=pltpu.CompilerParams(vmem_limit_bytes=52 << 20),
        cost_estimate=pl.CostEstimate(
            flops=2 * total * (2 * c * mid + 9 * mid**2),
            bytes_accessed=2 * (total * c + wr.size + ws.size + we.size + wm.size),
            transcendentals=0,
        ),
        name="encode",
    )(flat, wr, ws, we, wm)


def project_kernel(heads, spread_of, blocks, *refs):
    embs, (wq, wk, wv) = refs[:blocks], refs[blocks : blocks + 3]
    outs, scratch = refs[blocks + 3 : -1], refs[-1]
    a = lax.axis_index("blk") // spread_of
    values = jnp.concatenate([emb[...].astype(F32) for emb in embs], axis=0)
    rows = values.shape[0]
    center = jnp.mean(values, axis=1, keepdims=True)
    values = values - center
    spread = jnp.mean(values * values, axis=1, keepdims=True)
    normed = (values * lax.rsqrt(spread + 1e-05)).astype(BF16)
    query, key, value = (dot(normed, w[...]) for w in (wq, wk, wv))
    for head in range(heads):
        q, k, v = (r[:, head * HD : (head + 1) * HD] for r in (query, key, value))
        first = jnp.concatenate([q, v[:, 2 * THIRD :]], axis=1)
        second = jnp.concatenate([k, v[:, THIRD : 2 * THIRD]], axis=1)
        quarter = rows // 4
        third = jnp.concatenate([v[i * quarter : (i + 1) * quarter, :THIRD] for i in range(4)], axis=1)
        scratch[head] = jnp.concatenate([first, second, third], axis=0).astype(BF16)
    for e in range(heads):
        outs[e][...] = scratch[a ^ e]


def project(embs, wq, wk, wv, heads, spread_of):
    rows = embs[0].shape[0] * len(embs)
    packed = 2 * rows + rows // 4
    whole = pl.BlockSpec(memory_space=pltpu.VMEM)
    return pl.pallas_call(
        functools.partial(project_kernel, heads, spread_of, len(embs)),
        in_specs=[whole] * (len(embs) + 3),
        out_specs=[whole] * heads,
        out_shape=[jax.ShapeDtypeStruct((packed, LANES), BF16)] * heads,
        scratch_shapes=[pltpu.VMEM((heads, packed, LANES), BF16)],
        compiler_params=pltpu.CompilerParams(vmem_limit_bytes=24 << 20),
        cost_estimate=pl.CostEstimate(
            flops=6 * rows * wq.size, bytes_accessed=6 * wq.size, transcendentals=0
        ),
        name="project",
    )(*embs, wq, wk, wv)


def unpack_kernel(packs, *refs):
    query, key_value = refs[packs:]
    at = 0
    for pack in refs[:packs]:
        rows = pack.shape[0] * 4 // 9
        lane = lax.broadcasted_iota(jnp.int32, (rows, LANES), 1)
        first = pack[:rows].astype(F32)
        second = pack[rows : 2 * rows].astype(F32)
        third = pack[2 * rows :].astype(F32)
        low = jnp.concatenate(
            [third] + [pltpu.roll(third, LANES - i * THIRD, axis=1) for i in range(1, 4)], axis=0
        )
        middle = pltpu.roll(second, 2 * THIRD, axis=1)
        high = pltpu.roll(first, 3 * THIRD, axis=1)
        value = jnp.where(lane < THIRD, low, jnp.where(lane < 2 * THIRD, middle, high))
        value = jnp.where(lane < HD, value, jnp.where(lane == HD, 1.0, 0.0))
        key = jnp.where(lane < HD, second, 0.0)
        query[at : at + rows] = pack[:rows]
        key_value[at : at + rows, :LANES] = key.astype(BF16)
        key_value[at : at + rows, LANES:] = value.astype(BF16)
        at += rows


def unpack(packs):
    rows = sum(pack.shape[0] * 4 // 9 for pack in packs)
    whole = pl.BlockSpec(memory_space=pltpu.VMEM)
    return pl.pallas_call(
        functools.partial(unpack_kernel, len(packs)),
        in_specs=[whole] * len(packs),
        out_specs=[whole] * 2,
        out_shape=[
            jax.ShapeDtypeStruct((rows, LANES), BF16),
            jax.ShapeDtypeStruct((rows, 2 * LANES), BF16),
        ],
        compiler_params=pltpu.CompilerParams(vmem_limit_bytes=24 << 20),
        name="unpack",
    )(*packs)


class Layout:
    def __init__(self, slide_tiles, heads, spread_of, sets, count):
        blk = lax.axis_index("blk")
        self.t, self.a, self.c = lax.axis_index("tile"), blk // spread_of, lax.rem(blk, spread_of)
        self.spread_of, self.count = spread_of, count
        self.tiles_of = sum(len(members) for members in sets)
        self.blocks = [(e, d) for members in sets for e in range(heads) for d in members]
        first = slide_tiles[0]
        second = first + slide_tiles[1]
        self.ends = (first, second, second + slide_tiles[2])

    def starts(self, f):
        shards = [((self.a ^ e) * self.spread_of + (self.c ^ f), self.t ^ d) for e, d in self.blocks]
        return [(shard * self.tiles_of + tile) * self.count for shard, tile in shards]

    def slide_of(self, positions):
        return sum((positions >= end).astype(jnp.int32) for end in self.ends)

    def of_rows(self):
        row = lax.broadcasted_iota(jnp.int32, (self.count, 1), 0)
        return jnp.concatenate([self.slide_of(row + start) for start in self.starts(0)], axis=0)

    def of_keys(self, f):
        lane = lax.broadcasted_iota(jnp.int32, (1, len(self.blocks) * self.count), 1)
        starts = self.starts(f)
        positions = lane + starts[0]
        for i in range(1, len(starts)):
            step = starts[i] - starts[i - 1] - self.count
            positions = positions + jnp.where(lane >= i * self.count, step, 0)
        return self.slide_of(positions)


SCALE = math.log2(math.e) / math.sqrt(HD)


def masked_scores(query, keys, query_slide, key_slide):
    scores = lax.dot_general(query, keys, (((1,), (1,)), ((), ())), preferred_element_type=F32)
    return jnp.where(query_slide == key_slide, scores, -1e30)


def attend_own_kernel(layout, slide_tiles, queries, key_value, out):
    rows = layout(slide_tiles)
    query_slide, key_slide = rows.of_rows(), rows.of_keys(0)
    half = out.shape[0] // 2
    lane = lax.broadcasted_iota(jnp.int32, (half, LANES), 1)
    for at in (0, half):
        scores = masked_scores(
            queries[at : at + half], key_value[:, :LANES], query_slide[at : at + half], key_slide
        )
        top = jnp.max(scores, axis=1, keepdims=True)
        product = dot(jnp.exp2((scores - top) * SCALE).astype(BF16), key_value[:, LANES:])
        out[at : at + half] = jnp.where(lane == HD + 1, top, product)


def attend_others_kernel(layout, others_count, slide_tiles, queries, before, *refs):
    others, outs = refs[:others_count], refs[others_count:]
    rows = layout(slide_tiles)
    query_slide = rows.of_rows()
    key_slides = [rows.of_keys(f) for f in range(1, len(others) + 1)]
    half = query_slide.shape[0] // 2
    results = []
    for at in (0, half):
        scores = [
            masked_scores(queries[at : at + half], other[:, :LANES], query_slide[at : at + half], key_slide)
            for other, key_slide in zip(others, key_slides)
        ]
        own = before[at : at + half]
        top_own = own[:, HD + 1 : HD + 2]
        top = functools.reduce(jnp.maximum, [jnp.max(s, axis=1, keepdims=True) for s in scores], top_own)
        product = own * jnp.exp2((top_own - top) * SCALE)
        for other, s in zip(others, scores):
            product = product + dot(jnp.exp2((s - top) * SCALE).astype(BF16), other[:, LANES:])
        results.append(product[:, :HD] / product[:, HD : HD + 1])
    result = jnp.concatenate(results, axis=0)
    count = rows.count
    quarter = rows.tiles_of * count // 4
    for e in range(len(outs)):
        places = [rows.blocks.index((e, d)) * count for d in range(rows.tiles_of)]
        here = jnp.concatenate([result[at : at + count] for at in places], axis=0)
        rest = here[3 * quarter :]
        rest = jnp.concatenate([rest[:, i * THIRD : (i + 1) * THIRD] for i in range(3)], axis=0)
        outs[e][...] = jnp.concatenate([here[: 3 * quarter], rest], axis=1).astype(BF16)


def attend(slide_tiles, packs, heads, sets, count, exchange):
    queries, key_value = unpack(packs)
    rows = queries.shape[0]
    others = exchange(key_value)
    spread_of = len(others) + 1

    def layout(slide_tiles):
        return Layout(slide_tiles, heads, spread_of, sets, count)

    small = pl.BlockSpec(memory_space=pltpu.SMEM)
    whole = pl.BlockSpec(memory_space=pltpu.VMEM)
    params = pltpu.CompilerParams(vmem_limit_bytes=40 << 20)
    cost = pl.CostEstimate(
        flops=4 * rows * rows * LANES, bytes_accessed=6 * rows * LANES, transcendentals=rows * rows
    )
    partial = pl.pallas_call(
        functools.partial(attend_own_kernel, layout),
        in_specs=[small] + [whole] * 2,
        out_specs=whole,
        out_shape=jax.ShapeDtypeStruct((rows, LANES), F32),
        compiler_params=params,
        cost_estimate=cost,
        name="attend_own",
    )(slide_tiles, queries, key_value)
    packed = (rows // heads * 3 // 4, LANES)
    return pl.pallas_call(
        functools.partial(attend_others_kernel, layout, len(others)),
        in_specs=[small] + [whole] * (1 + spread_of),
        out_specs=[whole] * heads,
        out_shape=[jax.ShapeDtypeStruct(packed, BF16)] * heads,
        compiler_params=params,
        name="attend_others",
    )(slide_tiles, queries, partial, *others)


def partial_out_kernel(heads, tiles_of, spread_of, *refs):
    parts, w_out, outs = refs[:heads], refs[heads], refs[heads + 1 : heads + 1 + tiles_of]
    sorted_heads = refs[-1]
    a = lax.axis_index("blk") // spread_of
    quarter = parts[0].shape[0] // 3
    for e in range(heads):
        packed = parts[e][...].astype(F32)
        tail = packed[:, HD:]
        rest = jnp.concatenate([tail[i * quarter : (i + 1) * quarter] for i in range(3)], axis=1)
        sorted_heads[a ^ e] = jnp.concatenate([packed[:, :HD], rest], axis=0)
    attended = jnp.concatenate([sorted_heads[h] for h in range(heads)], axis=1).astype(BF16)
    product = dot(attended, w_out[...])
    count = product.shape[0] // tiles_of
    for d in range(tiles_of):
        outs[d][...] = product[d * count : (d + 1) * count].astype(outs[d].dtype)


def partial_out(parts, w_out, tiles_of, spread_of):
    heads, width = len(parts), w_out.shape[1]
    length = parts[0].shape[0] * 4 // 3
    count = length // tiles_of
    whole = pl.BlockSpec(memory_space=pltpu.VMEM)
    return pl.pallas_call(
        functools.partial(partial_out_kernel, heads, tiles_of, spread_of),
        in_specs=[whole] * (heads + 1),
        out_specs=[whole] * tiles_of,
        out_shape=[jax.ShapeDtypeStruct((count, width), F32 if d == 0 else BF16) for d in range(tiles_of)],
        scratch_shapes=[pltpu.VMEM((heads, length, HD), F32)],
        compiler_params=pltpu.CompilerParams(vmem_limit_bytes=24 << 20),
        name="partial_out",
    )(*parts, w_out)


def finish_kernel(emb, *refs):
    total = emb[...].astype(F32)
    for ref in refs[:-1]:
        total = total + ref[...].astype(F32)
    refs[-1][...] = total.astype(BF16)


def finish(emb, sums):
    return pl.pallas_call(
        finish_kernel,
        out_shape=jax.ShapeDtypeStruct(emb.shape, BF16),
        compiler_params=pltpu.CompilerParams(vmem_limit_bytes=24 << 20),
        name="finish",
    )(emb, *sums)


def shards(tiles_of, blks, tiles, wr, ws, we, wm, wq, wk, wv, wo, slide_tiles):
    count = tiles.shape[0]
    flat = tiles.reshape(count * SIDE * SIDE, tiles.shape[3])
    mid = wr.shape[1]
    heads = wq.shape[1] // HD
    spread_of = blks // heads

    def along(x, axis, size, step):
        return lax.ppermute(x, axis, [(i, i ^ step) for i in range(size)])

    def over_heads(blocks):
        return [blocks[0]] + [along(blocks[e], "blk", blks, e * spread_of) for e in range(1, heads)]

    emb = encode(flat, wr, ws.reshape(3, 3 * mid, mid), we, wm)
    embs = [emb] + [along(emb, "tile", tiles_of, d) for d in range(1, tiles_of)]
    sets = [range(tiles_of // 2), range(tiles_of // 2, tiles_of)]
    packs = []
    for members in sets:
        blocks = [embs[d] for d in members]
        if packs:
            *blocks, _ = lax.optimization_barrier((*blocks, packs[1]))
        packs += over_heads(project(blocks, wq, wk, wv, heads, spread_of))
    attended = attend(
        slide_tiles, packs, heads, sets, count,
        lambda x: [along(x, "blk", blks, f) for f in range(1, spread_of)],
    )
    sums = partial_out(over_heads(attended), wo, tiles_of, spread_of)
    sums = [sums[0]] + [along(sums[d], "tile", tiles_of, d) for d in range(1, tiles_of)]
    return finish(emb, sums)


def solution(mesh):
    placed = (
        P(("blk", "tile"), None, None, None),
        P(),
        P(),
        P(),
        P(),
        P(None, "tile"),
        P(None, "tile"),
        P(None, "tile"),
        P("tile", None),
        P(),
    )
    return jax.shard_map(
        functools.partial(shards, mesh.shape["tile"], mesh.shape["blk"]),
        mesh=mesh,
        in_specs=placed,
        out_specs=P(("blk", "tile"), None),
        check_vma=False,
    )
```

```python
import functools
import math

import jax
import jax.numpy as jnp
from jax import lax
from jax.experimental import pallas as pl
from jax.experimental.pallas import tpu as pltpu
from jax.sharding import PartitionSpec as P

SIDE = 8
HD = 96
THIRD = HD // 3
LANES = 128
F32 = jnp.float32
BF16 = jnp.bfloat16
GROUP = 16
PART = 16


def dot(a, b):
    return jnp.dot(a, b, preferred_element_type=F32)


def neighbours(rows):
    col = lax.broadcasted_iota(jnp.int32, rows.shape, 1)
    left = jnp.where(col >= 1, pltpu.roll(rows, 1, axis=1), 0.0)
    right = jnp.where(col <= SIDE - 2, pltpu.roll(rows, SIDE - 1, axis=1), 0.0)
    return left, rows, right


def row_combinations(d):
    even, odd = d[4] - 4.0 * d[2], d[3] - 4.0 * d[1]
    even2, odd2 = d[4] - d[2], 2.0 * (d[3] - d[1])
    return (
        d[0] - 1.25 * d[2] + 0.25 * d[4],
        even + odd,
        even - odd,
        even2 + odd2,
        even2 - odd2,
        4.0 * d[1] - 5.0 * d[3] + d[5],
    )


def tap_combinations(g):
    near, far = g[0] + g[2], g[0] + g[2] * 4
    double = g[1] * 2
    return near + g[1], near - g[1], far + double, far - double


def four_rows(m):
    near, near_odd = (m[1] + m[2]) * (-1 / 6), (m[1] - m[2]) * (-1 / 6)
    far, far_odd = (m[3] + m[4]) * (1 / 24), (m[3] - m[4]) * (1 / 24)
    return (
        m[0] + near + far,
        near_odd + 2.0 * far_odd,
        near + 4.0 * far,
        near_odd + 8.0 * far_odd + m[5],
    )


def encode_kernel(
    x_hbm, wr_hbm, ws_hbm, we_hbm, wm_hbm, emb,
    x, wr, ws, we, mixed_taps, reduced, products, pooled, x_sems, tap_sems, sems,
):
    step = pl.program_id(0)
    count, c = pooled.shape
    area = SIDE * SIDE
    mid = wr.shape[1]
    groups = count // GROUP
    per = GROUP // PART
    parts = groups * per
    early = 2 * per
    chunk = 3 * mid // early
    last = 2 * groups - 1

    def x_copy(g):
        at = pl.ds(pl.multiple_of(g * PART * area, PART * area), PART * area)
        return pltpu.make_async_copy(x_hbm.at[at], x.at[at], x_sems.at[g])

    def tap_copy(g):
        at = pl.ds(pl.multiple_of(g * chunk, chunk), chunk)
        return pltpu.make_async_copy(ws_hbm.at[:, at], ws.at[:, at], tap_sems.at[g])

    wm = x.at[: wm_hbm.shape[0], : wm_hbm.shape[1]]
    wr_copy, we_copy, wm_copy = (
        pltpu.make_async_copy(src, dst, sems.at[i])
        for i, (src, dst) in enumerate(((wr_hbm, wr), (we_hbm, we), (wm_hbm, wm)))
    )

    @pl.when(step == 0)
    def _():
        x_copy(0).start()
        wr_copy.start()
        x_copy(1).start()
        tap_copy(0).start()
        wr_copy.wait()

    @pl.when((step == 0) | ((lax.rem(step, 2) == 1) & (step < last)))
    def _():
        @pl.loop(0, per)
        def _(i):
            g = (step + 1) // 2 * per + i
            x_copy(g).wait()

            @pl.when(g + 2 < parts)
            def _():
                x_copy(g + 2).start()

            @pl.when(g + 1 < early)
            def _():
                tap_copy(g + 1).start()

            @pl.when(g == early - 1)
            def _():
                we_copy.start()

            rows = x[pl.ds(pl.multiple_of(g * PART * area, PART * area), PART * area), :]
            maps = jnp.maximum(dot(rows, wr[...]), 0.0).reshape(PART, SIDE, SIDE, mid)
            reduced[:, pl.ds(pl.multiple_of(g * PART, PART), PART)] = maps.swapaxes(0, 1)

            @pl.when(g < early)
            def _():
                tap_copy(g).wait()
                at = pl.ds(pl.multiple_of(g * chunk, chunk), chunk)
                for k, taps in enumerate(tap_combinations([ws[dy, at, :] for dy in range(3)])):
                    mixed_taps[k, at, :] = taps

    @pl.when(step == 2)
    def _():
        we_copy.wait()

    @pl.when(step == last)
    def _():
        wm_copy.start()

    @pl.when(((lax.rem(step, 2) == 0) & (step > 0)) | (step == last))
    def _():
        g = jnp.where(step == last, groups - 1, step // 2 - 1)
        band = GROUP * SIDE
        maps = reduced[:, pl.ds(pl.multiple_of(g * GROUP, GROUP), GROUP)].reshape(SIDE, band, mid)
        edge = jnp.zeros((band, mid), F32)
        d = [edge] + [maps[i] for i in range(SIDE)] + [edge]
        upper, lower = row_combinations(d[0:6]), row_combinations(d[4:10])
        taps = [ws.at[0]] + [mixed_taps.at[k] for k in range(4)] + [ws.at[2]]
        for k in range(6):
            both = jnp.concatenate([upper[k], lower[k]], axis=0).reshape(2 * GROUP, SIDE, mid)
            window = [p.reshape(2 * band, mid).astype(BF16) for p in neighbours(both)]
            products[k] = dot(jnp.concatenate(window, axis=1), taps[k][...])
        rows = four_rows([products[k, :band] for k in range(6)])
        rows += four_rows([products[k, band:] for k in range(6)])
        spatial = jnp.stack([jnp.maximum(r, 0.0).reshape(GROUP, SIDE, mid) for r in rows], axis=0)
        spatial = spatial.swapaxes(0, 1).reshape(GROUP * area, mid).astype(BF16)
        at = pl.ds(pl.multiple_of(g * GROUP * area, GROUP * area), GROUP * area)
        out = jnp.maximum(dot(spatial, we[...]) + x[at, :].astype(F32), 0.0)
        mean = jnp.sum(out.reshape(GROUP, area, c), axis=1) * (1.0 / area)
        pooled[pl.ds(pl.multiple_of(g * GROUP, GROUP), GROUP), :] = mean

    @pl.when(step == last)
    def _():
        wm_copy.wait()
        emb[...] = dot(pooled[...].astype(BF16), wm[...]).astype(BF16)


def encode(flat, wr, ws, we, wm):
    total, c = flat.shape
    count = total // (SIDE * SIDE)
    assert wm.shape[0] <= total - GROUP * SIDE * SIDE and wm.shape[1] <= c
    mid = wr.shape[1]
    return pl.pallas_call(
        encode_kernel,
        grid=(2 * count // GROUP,),
        in_specs=[pl.BlockSpec(memory_space=pl.ANY)] * 5,
        out_specs=pl.BlockSpec((count, wm.shape[1]), lambda i: (0, 0)),
        out_shape=jax.ShapeDtypeStruct((count, wm.shape[1]), BF16),
        scratch_shapes=[
            pltpu.VMEM(flat.shape, BF16),
            pltpu.VMEM(wr.shape, BF16),
            pltpu.VMEM(ws.shape, BF16),
            pltpu.VMEM(we.shape, BF16),
            pltpu.VMEM((4,) + ws.shape[1:], BF16),
            pltpu.VMEM((SIDE, count, SIDE, mid), F32),
            pltpu.VMEM((6, 2 * GROUP * SIDE, mid), F32),
            pltpu.VMEM((count, c), F32),
            pltpu.SemaphoreType.DMA((count // PART,)),
            pltpu.SemaphoreType.DMA((2 * GROUP // PART,)),
            pltpu.SemaphoreType.DMA((3,)),
        ],
        compiler_params=pltpu.CompilerParams(vmem_limit_bytes=52 << 20),
        cost_estimate=pl.CostEstimate(
            flops=2 * total * (2 * c * mid + 9 * mid**2),
            bytes_accessed=2 * (total * c + wr.size + ws.size + we.size + wm.size),
            transcendentals=0,
        ),
        name="encode",
    )(flat, wr, ws, we, wm)


def project_kernel(heads, spread_of, blocks, *refs):
    embs, (wq, wk, wv) = refs[:blocks], refs[blocks : blocks + 3]
    outs, scratch = refs[blocks + 3 : -1], refs[-1]
    a = lax.axis_index("blk") // spread_of
    values = jnp.concatenate([emb[...].astype(F32) for emb in embs], axis=0)
    rows = values.shape[0]
    center = jnp.mean(values, axis=1, keepdims=True)
    values = values - center
    spread = jnp.mean(values * values, axis=1, keepdims=True)
    normed = (values * lax.rsqrt(spread + 1e-05)).astype(BF16)
    query, key, value = (dot(normed, w[...]) for w in (wq, wk, wv))
    for head in range(heads):
        q, k, v = (r[:, head * HD : (head + 1) * HD] for r in (query, key, value))
        first = jnp.concatenate([q, v[:, 2 * THIRD :]], axis=1)
        second = jnp.concatenate([k, v[:, THIRD : 2 * THIRD]], axis=1)
        quarter = rows // 4
        third = jnp.concatenate([v[i * quarter : (i + 1) * quarter, :THIRD] for i in range(4)], axis=1)
        scratch[head] = jnp.concatenate([first, second, third], axis=0).astype(BF16)
    for e in range(heads):
        outs[e][...] = scratch[a ^ e]


def project(embs, wq, wk, wv, heads, spread_of):
    rows = embs[0].shape[0] * len(embs)
    packed = 2 * rows + rows // 4
    whole = pl.BlockSpec(memory_space=pltpu.VMEM)
    return pl.pallas_call(
        functools.partial(project_kernel, heads, spread_of, len(embs)),
        in_specs=[whole] * (len(embs) + 3),
        out_specs=[whole] * heads,
        out_shape=[jax.ShapeDtypeStruct((packed, LANES), BF16)] * heads,
        scratch_shapes=[pltpu.VMEM((heads, packed, LANES), BF16)],
        compiler_params=pltpu.CompilerParams(vmem_limit_bytes=24 << 20),
        cost_estimate=pl.CostEstimate(
            flops=6 * rows * wq.size, bytes_accessed=6 * wq.size, transcendentals=0
        ),
        name="project",
    )(*embs, wq, wk, wv)


def unpack_kernel(packs, *refs):
    query, key_value = refs[packs:]
    at = 0
    for pack in refs[:packs]:
        rows = pack.shape[0] * 4 // 9
        lane = lax.broadcasted_iota(jnp.int32, (rows, LANES), 1)
        first = pack[:rows].astype(F32)
        second = pack[rows : 2 * rows].astype(F32)
        third = pack[2 * rows :].astype(F32)
        low = jnp.concatenate(
            [third] + [pltpu.roll(third, LANES - i * THIRD, axis=1) for i in range(1, 4)], axis=0
        )
        middle = pltpu.roll(second, 2 * THIRD, axis=1)
        high = pltpu.roll(first, 3 * THIRD, axis=1)
        value = jnp.where(lane < THIRD, low, jnp.where(lane < 2 * THIRD, middle, high))
        value = jnp.where(lane < HD, value, jnp.where(lane == HD, 1.0, 0.0))
        key = jnp.where(lane < HD, second, 0.0)
        query[at : at + rows] = pack[:rows]
        key_value[at : at + rows, :LANES] = key.astype(BF16)
        key_value[at : at + rows, LANES:] = value.astype(BF16)
        at += rows


def unpack(packs):
    rows = sum(pack.shape[0] * 4 // 9 for pack in packs)
    whole = pl.BlockSpec(memory_space=pltpu.VMEM)
    return pl.pallas_call(
        functools.partial(unpack_kernel, len(packs)),
        in_specs=[whole] * len(packs),
        out_specs=[whole] * 2,
        out_shape=[
            jax.ShapeDtypeStruct((rows, LANES), BF16),
            jax.ShapeDtypeStruct((rows, 2 * LANES), BF16),
        ],
        compiler_params=pltpu.CompilerParams(vmem_limit_bytes=24 << 20),
        name="unpack",
    )(*packs)


class Layout:
    def __init__(self, slide_tiles, heads, spread_of, sets, count):
        blk = lax.axis_index("blk")
        self.t, self.a, self.c = lax.axis_index("tile"), blk // spread_of, lax.rem(blk, spread_of)
        self.spread_of, self.count = spread_of, count
        self.tiles_of = sum(len(members) for members in sets)
        self.blocks = [(e, d) for members in sets for e in range(heads) for d in members]
        first = slide_tiles[0]
        second = first + slide_tiles[1]
        self.ends = (first, second, second + slide_tiles[2])

    def starts(self, f):
        shards = [((self.a ^ e) * self.spread_of + (self.c ^ f), self.t ^ d) for e, d in self.blocks]
        return [(shard * self.tiles_of + tile) * self.count for shard, tile in shards]

    def slide_of(self, positions):
        return sum((positions >= end).astype(jnp.int32) for end in self.ends)

    def of_rows(self):
        row = lax.broadcasted_iota(jnp.int32, (self.count, 1), 0)
        return jnp.concatenate([self.slide_of(row + start) for start in self.starts(0)], axis=0)

    def of_keys(self, f):
        lane = lax.broadcasted_iota(jnp.int32, (1, len(self.blocks) * self.count), 1)
        starts = self.starts(f)
        positions = lane + starts[0]
        for i in range(1, len(starts)):
            step = starts[i] - starts[i - 1] - self.count
            positions = positions + jnp.where(lane >= i * self.count, step, 0)
        return self.slide_of(positions)


SCALE = math.log2(math.e) / math.sqrt(HD)


def masked_scores(query, keys, query_slide, key_slide):
    scores = lax.dot_general(query, keys, (((1,), (1,)), ((), ())), preferred_element_type=F32)
    return jnp.where(query_slide == key_slide, scores, -1e30)


def attend_own_kernel(layout, slide_tiles, queries, key_value, out):
    rows = layout(slide_tiles)
    query_slide, key_slide = rows.of_rows(), rows.of_keys(0)
    half = out.shape[0] // 2
    lane = lax.broadcasted_iota(jnp.int32, (half, LANES), 1)
    for at in (0, half):
        scores = masked_scores(
            queries[at : at + half], key_value[:, :LANES], query_slide[at : at + half], key_slide
        )
        top = jnp.max(scores, axis=1, keepdims=True)
        product = dot(jnp.exp2((scores - top) * SCALE).astype(BF16), key_value[:, LANES:])
        out[at : at + half] = jnp.where(lane == HD + 1, top, product)


def attend_others_kernel(layout, others_count, slide_tiles, queries, before, *refs):
    others, outs = refs[:others_count], refs[others_count:]
    rows = layout(slide_tiles)
    query_slide = rows.of_rows()
    key_slides = [rows.of_keys(f) for f in range(1, len(others) + 1)]
    half = query_slide.shape[0] // 2
    results = []
    for at in (0, half):
        scores = [
            masked_scores(queries[at : at + half], other[:, :LANES], query_slide[at : at + half], key_slide)
            for other, key_slide in zip(others, key_slides)
        ]
        own = before[at : at + half]
        top_own = own[:, HD + 1 : HD + 2]
        top = functools.reduce(jnp.maximum, [jnp.max(s, axis=1, keepdims=True) for s in scores], top_own)
        product = own * jnp.exp2((top_own - top) * SCALE)
        for other, s in zip(others, scores):
            product = product + dot(jnp.exp2((s - top) * SCALE).astype(BF16), other[:, LANES:])
        results.append(product[:, :HD] / product[:, HD : HD + 1])
    result = jnp.concatenate(results, axis=0)
    count = rows.count
    quarter = rows.tiles_of * count // 4
    for e in range(len(outs)):
        places = [rows.blocks.index((e, d)) * count for d in range(rows.tiles_of)]
        here = jnp.concatenate([result[at : at + count] for at in places], axis=0)
        rest = here[3 * quarter :]
        rest = jnp.concatenate([rest[:, i * THIRD : (i + 1) * THIRD] for i in range(3)], axis=0)
        outs[e][...] = jnp.concatenate([here[: 3 * quarter], rest], axis=1).astype(BF16)


def attend(slide_tiles, packs, heads, sets, count, exchange):
    queries, key_value = unpack(packs)
    rows = queries.shape[0]
    others = exchange(key_value)
    spread_of = len(others) + 1

    def layout(slide_tiles):
        return Layout(slide_tiles, heads, spread_of, sets, count)

    small = pl.BlockSpec(memory_space=pltpu.SMEM)
    whole = pl.BlockSpec(memory_space=pltpu.VMEM)
    params = pltpu.CompilerParams(vmem_limit_bytes=40 << 20)
    cost = pl.CostEstimate(
        flops=4 * rows * rows * LANES, bytes_accessed=6 * rows * LANES, transcendentals=rows * rows
    )
    partial = pl.pallas_call(
        functools.partial(attend_own_kernel, layout),
        in_specs=[small] + [whole] * 2,
        out_specs=whole,
        out_shape=jax.ShapeDtypeStruct((rows, LANES), F32),
        compiler_params=params,
        cost_estimate=cost,
        name="attend_own",
    )(slide_tiles, queries, key_value)
    packed = (rows // heads * 3 // 4, LANES)
    return pl.pallas_call(
        functools.partial(attend_others_kernel, layout, len(others)),
        in_specs=[small] + [whole] * (1 + spread_of),
        out_specs=[whole] * heads,
        out_shape=[jax.ShapeDtypeStruct(packed, BF16)] * heads,
        compiler_params=params,
        name="attend_others",
    )(slide_tiles, queries, partial, *others)


def partial_out_kernel(heads, tiles_of, spread_of, *refs):
    parts, w_out, outs = refs[:heads], refs[heads], refs[heads + 1 : heads + 1 + tiles_of]
    sorted_heads = refs[-1]
    a = lax.axis_index("blk") // spread_of
    quarter = parts[0].shape[0] // 3
    for e in range(heads):
        packed = parts[e][...].astype(F32)
        tail = packed[:, HD:]
        rest = jnp.concatenate([tail[i * quarter : (i + 1) * quarter] for i in range(3)], axis=1)
        sorted_heads[a ^ e] = jnp.concatenate([packed[:, :HD], rest], axis=0)
    attended = jnp.concatenate([sorted_heads[h] for h in range(heads)], axis=1).astype(BF16)
    product = dot(attended, w_out[...])
    count = product.shape[0] // tiles_of
    for d in range(tiles_of):
        outs[d][...] = product[d * count : (d + 1) * count].astype(outs[d].dtype)


def partial_out(parts, w_out, tiles_of, spread_of):
    heads, width = len(parts), w_out.shape[1]
    length = parts[0].shape[0] * 4 // 3
    count = length // tiles_of
    whole = pl.BlockSpec(memory_space=pltpu.VMEM)
    return pl.pallas_call(
        functools.partial(partial_out_kernel, heads, tiles_of, spread_of),
        in_specs=[whole] * (heads + 1),
        out_specs=[whole] * tiles_of,
        out_shape=[jax.ShapeDtypeStruct((count, width), F32 if d == 0 else BF16) for d in range(tiles_of)],
        scratch_shapes=[pltpu.VMEM((heads, length, HD), F32)],
        compiler_params=pltpu.CompilerParams(vmem_limit_bytes=24 << 20),
        name="partial_out",
    )(*parts, w_out)


def finish_kernel(emb, *refs):
    total = emb[...].astype(F32)
    for ref in refs[:-1]:
        total = total + ref[...].astype(F32)
    refs[-1][...] = total.astype(BF16)


def finish(emb, sums):
    return pl.pallas_call(
        finish_kernel,
        out_shape=jax.ShapeDtypeStruct(emb.shape, BF16),
        compiler_params=pltpu.CompilerParams(vmem_limit_bytes=24 << 20),
        name="finish",
    )(emb, *sums)


def shards(tiles_of, blks, tiles, wr, ws, we, wm, wq, wk, wv, wo, slide_tiles):
    count = tiles.shape[0]
    flat = tiles.reshape(count * SIDE * SIDE, tiles.shape[3])
    mid = wr.shape[1]
    heads = wq.shape[1] // HD
    spread_of = blks // heads

    def along(x, axis, size, step):
        return lax.ppermute(x, axis, [(i, i ^ step) for i in range(size)])

    def over_heads(blocks):
        return [blocks[0]] + [along(blocks[e], "blk", blks, e * spread_of) for e in range(1, heads)]

    emb = encode(flat, wr, ws.reshape(3, 3 * mid, mid), we, wm)
    embs = [emb] + [along(emb, "tile", tiles_of, d) for d in range(1, tiles_of)]
    sets = [range(tiles_of // 2), range(tiles_of // 2, tiles_of)]
    packs = []
    for members in sets:
        blocks = [embs[d] for d in members]
        if packs:
            *blocks, _ = lax.optimization_barrier((*blocks, packs[1]))
        packs += over_heads(project(blocks, wq, wk, wv, heads, spread_of))
    attended = attend(
        slide_tiles, packs, heads, sets, count,
        lambda x: [along(x, "blk", blks, f) for f in range(1, spread_of)],
    )
    sums = partial_out(over_heads(attended), wo, tiles_of, spread_of)
    sums = [sums[0]] + [along(sums[d], "tile", tiles_of, d) for d in range(1, tiles_of)]
    return finish(emb, sums)


def solution(mesh):
    placed = (
        P(("blk", "tile"), None, None, None),
        P(),
        P(),
        P(),
        P(),
        P(None, "tile"),
        P(None, "tile"),
        P(None, "tile"),
        P("tile", None),
        P(),
    )
    return jax.shard_map(
        functools.partial(shards, mesh.shape["tile"], mesh.shape["blk"]),
        mesh=mesh,
        in_specs=placed,
        out_specs=P(("blk", "tile"), None),
        check_vma=False,
    )
```

```python
import functools
import math

import jax
import jax.numpy as jnp
from jax import lax
from jax.experimental import pallas as pl
from jax.experimental.pallas import tpu as pltpu
from jax.sharding import PartitionSpec as P

SIDE = 8
HD = 96
THIRD = HD // 3
LANES = 128
F32 = jnp.float32
BF16 = jnp.bfloat16
GROUP = 16
PART = 16


def dot(a, b):
    return jnp.dot(a, b, preferred_element_type=F32)


def neighbours(rows):
    col = lax.broadcasted_iota(jnp.int32, rows.shape, 1)
    left = jnp.where(col >= 1, pltpu.roll(rows, 1, axis=1), 0.0)
    right = jnp.where(col <= SIDE - 2, pltpu.roll(rows, SIDE - 1, axis=1), 0.0)
    return left, rows, right


def row_combinations(d):
    even, odd = d[4] - 4.0 * d[2], d[3] - 4.0 * d[1]
    even2, odd2 = d[4] - d[2], 2.0 * (d[3] - d[1])
    return (
        d[0] - 1.25 * d[2] + 0.25 * d[4],
        even + odd,
        even - odd,
        even2 + odd2,
        even2 - odd2,
        4.0 * d[1] - 5.0 * d[3] + d[5],
    )


def tap_combinations(g):
    near, far = g[0] + g[2], g[0] + g[2] * 4
    double = g[1] * 2
    return near + g[1], near - g[1], far + double, far - double


def four_rows(m):
    near, near_odd = (m[1] + m[2]) * (-1 / 6), (m[1] - m[2]) * (-1 / 6)
    far, far_odd = (m[3] + m[4]) * (1 / 24), (m[3] - m[4]) * (1 / 24)
    return (
        m[0] + near + far,
        near_odd + 2.0 * far_odd,
        near + 4.0 * far,
        near_odd + 8.0 * far_odd + m[5],
    )


def encode_kernel(
    x_hbm, wr_hbm, ws_hbm, we_hbm, wm_hbm, emb,
    x, wr, ws, we, mixed_taps, reduced, products, pooled, x_sems, tap_sems, sems,
):
    step = pl.program_id(0)
    count, c = pooled.shape
    area = SIDE * SIDE
    mid = wr.shape[1]
    groups = count // GROUP
    per = GROUP // PART
    parts = groups * per
    early = 2 * per
    chunk = 3 * mid // early
    last = 2 * groups - 1

    def x_copy(g):
        at = pl.ds(pl.multiple_of(g * PART * area, PART * area), PART * area)
        return pltpu.make_async_copy(x_hbm.at[at], x.at[at], x_sems.at[g])

    def tap_copy(g):
        at = pl.ds(pl.multiple_of(g * chunk, chunk), chunk)
        return pltpu.make_async_copy(ws_hbm.at[:, at], ws.at[:, at], tap_sems.at[g])

    wm = x.at[: wm_hbm.shape[0], : wm_hbm.shape[1]]
    wr_copy, we_copy, wm_copy = (
        pltpu.make_async_copy(src, dst, sems.at[i])
        for i, (src, dst) in enumerate(((wr_hbm, wr), (we_hbm, we), (wm_hbm, wm)))
    )

    @pl.when(step == 0)
    def _():
        x_copy(0).start()
        wr_copy.start()
        x_copy(1).start()
        tap_copy(0).start()
        wr_copy.wait()

    @pl.when((step == 0) | ((lax.rem(step, 2) == 1) & (step < last)))
    def _():
        @pl.loop(0, per)
        def _(i):
            g = (step + 1) // 2 * per + i
            x_copy(g).wait()

            @pl.when((g >= 1) & (g + 1 < parts))
            def _():
                x_copy(g + 1).start()

            @pl.when(g + 1 < early)
            def _():
                tap_copy(g + 1).start()

            @pl.when(g == early - 1)
            def _():
                we_copy.start()

            rows = x[pl.ds(pl.multiple_of(g * PART * area, PART * area), PART * area), :]
            maps = jnp.maximum(dot(rows, wr[...]), 0.0).reshape(PART, SIDE, SIDE, mid)
            reduced[:, pl.ds(pl.multiple_of(g * PART, PART), PART)] = maps.swapaxes(0, 1)

            @pl.when(g < early)
            def _():
                tap_copy(g).wait()
                at = pl.ds(pl.multiple_of(g * chunk, chunk), chunk)
                for k, taps in enumerate(tap_combinations([ws[dy, at, :] for dy in range(3)])):
                    mixed_taps[k, at, :] = taps

    @pl.when(step == 2)
    def _():
        we_copy.wait()

    @pl.when(step == last)
    def _():
        wm_copy.start()

    @pl.when(((lax.rem(step, 2) == 0) & (step > 0)) | (step == last))
    def _():
        g = jnp.where(step == last, groups - 1, step // 2 - 1)
        band = GROUP * SIDE
        maps = reduced[:, pl.ds(pl.multiple_of(g * GROUP, GROUP), GROUP)].reshape(SIDE, band, mid)
        edge = jnp.zeros((band, mid), F32)
        d = [edge] + [maps[i] for i in range(SIDE)] + [edge]
        upper, lower = row_combinations(d[0:6]), row_combinations(d[4:10])
        taps = [ws.at[0]] + [mixed_taps.at[k] for k in range(4)] + [ws.at[2]]
        for k in range(6):
            both = jnp.concatenate([upper[k], lower[k]], axis=0).reshape(2 * GROUP, SIDE, mid)
            window = [p.reshape(2 * band, mid).astype(BF16) for p in neighbours(both)]
            products[k] = dot(jnp.concatenate(window, axis=1), taps[k][...])
        rows = four_rows([products[k, :band] for k in range(6)])
        rows += four_rows([products[k, band:] for k in range(6)])
        spatial = jnp.stack([jnp.maximum(r, 0.0).reshape(GROUP, SIDE, mid) for r in rows], axis=0)
        spatial = spatial.swapaxes(0, 1).reshape(GROUP * area, mid).astype(BF16)
        at = pl.ds(pl.multiple_of(g * GROUP * area, GROUP * area), GROUP * area)
        out = jnp.maximum(dot(spatial, we[...]) + x[at, :].astype(F32), 0.0)
        mean = jnp.sum(out.reshape(GROUP, area, c), axis=1) * (1.0 / area)
        pooled[pl.ds(pl.multiple_of(g * GROUP, GROUP), GROUP), :] = mean

    @pl.when(step == last)
    def _():
        wm_copy.wait()
        emb[...] = dot(pooled[...].astype(BF16), wm[...]).astype(BF16)


def encode(flat, wr, ws, we, wm):
    total, c = flat.shape
    count = total // (SIDE * SIDE)
    assert wm.shape[0] <= total - GROUP * SIDE * SIDE and wm.shape[1] <= c
    mid = wr.shape[1]
    return pl.pallas_call(
        encode_kernel,
        grid=(2 * count // GROUP,),
        in_specs=[pl.BlockSpec(memory_space=pl.ANY)] * 5,
        out_specs=pl.BlockSpec((count, wm.shape[1]), lambda i: (0, 0)),
        out_shape=jax.ShapeDtypeStruct((count, wm.shape[1]), BF16),
        scratch_shapes=[
            pltpu.VMEM(flat.shape, BF16),
            pltpu.VMEM(wr.shape, BF16),
            pltpu.VMEM(ws.shape, BF16),
            pltpu.VMEM(we.shape, BF16),
            pltpu.VMEM((4,) + ws.shape[1:], BF16),
            pltpu.VMEM((SIDE, count, SIDE, mid), F32),
            pltpu.VMEM((6, 2 * GROUP * SIDE, mid), F32),
            pltpu.VMEM((count, c), F32),
            pltpu.SemaphoreType.DMA((count // PART,)),
            pltpu.SemaphoreType.DMA((2 * GROUP // PART,)),
            pltpu.SemaphoreType.DMA((3,)),
        ],
        compiler_params=pltpu.CompilerParams(vmem_limit_bytes=52 << 20),
        cost_estimate=pl.CostEstimate(
            flops=2 * total * (2 * c * mid + 9 * mid**2),
            bytes_accessed=2 * (total * c + wr.size + ws.size + we.size + wm.size),
            transcendentals=0,
        ),
        name="encode",
    )(flat, wr, ws, we, wm)


def project_kernel(heads, spread_of, blocks, *refs):
    embs, (wq, wk, wv) = refs[:blocks], refs[blocks : blocks + 3]
    outs, scratch = refs[blocks + 3 : -1], refs[-1]
    a = lax.axis_index("blk") // spread_of
    values = jnp.concatenate([emb[...].astype(F32) for emb in embs], axis=0)
    rows = values.shape[0]
    center = jnp.mean(values, axis=1, keepdims=True)
    values = values - center
    spread = jnp.mean(values * values, axis=1, keepdims=True)
    normed = (values * lax.rsqrt(spread + 1e-05)).astype(BF16)
    query, key, value = (dot(normed, w[...]) for w in (wq, wk, wv))
    for head in range(heads):
        q, k, v = (r[:, head * HD : (head + 1) * HD] for r in (query, key, value))
        first = jnp.concatenate([q, v[:, 2 * THIRD :]], axis=1)
        second = jnp.concatenate([k, v[:, THIRD : 2 * THIRD]], axis=1)
        quarter = rows // 4
        third = jnp.concatenate([v[i * quarter : (i + 1) * quarter, :THIRD] for i in range(4)], axis=1)
        scratch[head] = jnp.concatenate([first, second, third], axis=0).astype(BF16)
    for e in range(heads):
        outs[e][...] = scratch[a ^ e]


def project(embs, wq, wk, wv, heads, spread_of):
    rows = embs[0].shape[0] * len(embs)
    packed = 2 * rows + rows // 4
    whole = pl.BlockSpec(memory_space=pltpu.VMEM)
    return pl.pallas_call(
        functools.partial(project_kernel, heads, spread_of, len(embs)),
        in_specs=[whole] * (len(embs) + 3),
        out_specs=[whole] * heads,
        out_shape=[jax.ShapeDtypeStruct((packed, LANES), BF16)] * heads,
        scratch_shapes=[pltpu.VMEM((heads, packed, LANES), BF16)],
        compiler_params=pltpu.CompilerParams(vmem_limit_bytes=24 << 20),
        cost_estimate=pl.CostEstimate(
            flops=6 * rows * wq.size, bytes_accessed=6 * wq.size, transcendentals=0
        ),
        name="project",
    )(*embs, wq, wk, wv)


def unpack_kernel(packs, *refs):
    query, key_value = refs[packs:]
    at = 0
    for pack in refs[:packs]:
        rows = pack.shape[0] * 4 // 9
        lane = lax.broadcasted_iota(jnp.int32, (rows, LANES), 1)
        first = pack[:rows].astype(F32)
        second = pack[rows : 2 * rows].astype(F32)
        third = pack[2 * rows :].astype(F32)
        low = jnp.concatenate(
            [third] + [pltpu.roll(third, LANES - i * THIRD, axis=1) for i in range(1, 4)], axis=0
        )
        middle = pltpu.roll(second, 2 * THIRD, axis=1)
        high = pltpu.roll(first, 3 * THIRD, axis=1)
        value = jnp.where(lane < THIRD, low, jnp.where(lane < 2 * THIRD, middle, high))
        value = jnp.where(lane < HD, value, jnp.where(lane == HD, 1.0, 0.0))
        key = jnp.where(lane < HD, second, 0.0)
        query[at : at + rows] = pack[:rows]
        key_value[at : at + rows, :LANES] = key.astype(BF16)
        key_value[at : at + rows, LANES:] = value.astype(BF16)
        at += rows


def unpack(packs):
    rows = sum(pack.shape[0] * 4 // 9 for pack in packs)
    whole = pl.BlockSpec(memory_space=pltpu.VMEM)
    return pl.pallas_call(
        functools.partial(unpack_kernel, len(packs)),
        in_specs=[whole] * len(packs),
        out_specs=[whole] * 2,
        out_shape=[
            jax.ShapeDtypeStruct((rows, LANES), BF16),
            jax.ShapeDtypeStruct((rows, 2 * LANES), BF16),
        ],
        compiler_params=pltpu.CompilerParams(vmem_limit_bytes=24 << 20),
        name="unpack",
    )(*packs)


class Layout:
    def __init__(self, slide_tiles, heads, spread_of, sets, count):
        blk = lax.axis_index("blk")
        self.t, self.a, self.c = lax.axis_index("tile"), blk // spread_of, lax.rem(blk, spread_of)
        self.spread_of, self.count = spread_of, count
        self.tiles_of = sum(len(members) for members in sets)
        self.blocks = [(e, d) for members in sets for e in range(heads) for d in members]
        first = slide_tiles[0]
        second = first + slide_tiles[1]
        self.ends = (first, second, second + slide_tiles[2])

    def starts(self, f):
        shards = [((self.a ^ e) * self.spread_of + (self.c ^ f), self.t ^ d) for e, d in self.blocks]
        return [(shard * self.tiles_of + tile) * self.count for shard, tile in shards]

    def slide_of(self, positions):
        return sum((positions >= end).astype(jnp.int32) for end in self.ends)

    def of_rows(self):
        row = lax.broadcasted_iota(jnp.int32, (self.count, 1), 0)
        return jnp.concatenate([self.slide_of(row + start) for start in self.starts(0)], axis=0)

    def of_keys(self, f):
        lane = lax.broadcasted_iota(jnp.int32, (1, len(self.blocks) * self.count), 1)
        starts = self.starts(f)
        positions = lane + starts[0]
        for i in range(1, len(starts)):
            step = starts[i] - starts[i - 1] - self.count
            positions = positions + jnp.where(lane >= i * self.count, step, 0)
        return self.slide_of(positions)


SCALE = math.log2(math.e) / math.sqrt(HD)


def masked_scores(query, keys, query_slide, key_slide):
    scores = lax.dot_general(query, keys, (((1,), (1,)), ((), ())), preferred_element_type=F32)
    return jnp.where(query_slide == key_slide, scores, -1e30)


def attend_own_kernel(layout, slide_tiles, queries, key_value, out):
    rows = layout(slide_tiles)
    query_slide, key_slide = rows.of_rows(), rows.of_keys(0)
    half = out.shape[0] // 2
    lane = lax.broadcasted_iota(jnp.int32, (half, LANES), 1)
    for at in (0, half):
        scores = masked_scores(
            queries[at : at + half], key_value[:, :LANES], query_slide[at : at + half], key_slide
        )
        top = jnp.max(scores, axis=1, keepdims=True)
        product = dot(jnp.exp2((scores - top) * SCALE).astype(BF16), key_value[:, LANES:])
        out[at : at + half] = jnp.where(lane == HD + 1, top, product)


def attend_others_kernel(layout, others_count, slide_tiles, queries, before, *refs):
    others, outs = refs[:others_count], refs[others_count:]
    rows = layout(slide_tiles)
    query_slide = rows.of_rows()
    key_slides = [rows.of_keys(f) for f in range(1, len(others) + 1)]
    half = query_slide.shape[0] // 2
    results = []
    for at in (0, half):
        scores = [
            masked_scores(queries[at : at + half], other[:, :LANES], query_slide[at : at + half], key_slide)
            for other, key_slide in zip(others, key_slides)
        ]
        own = before[at : at + half]
        top_own = own[:, HD + 1 : HD + 2]
        top = functools.reduce(jnp.maximum, [jnp.max(s, axis=1, keepdims=True) for s in scores], top_own)
        product = own * jnp.exp2((top_own - top) * SCALE)
        for other, s in zip(others, scores):
            product = product + dot(jnp.exp2((s - top) * SCALE).astype(BF16), other[:, LANES:])
        results.append(product[:, :HD] / product[:, HD : HD + 1])
    result = jnp.concatenate(results, axis=0)
    count = rows.count
    quarter = rows.tiles_of * count // 4
    for e in range(len(outs)):
        places = [rows.blocks.index((e, d)) * count for d in range(rows.tiles_of)]
        here = jnp.concatenate([result[at : at + count] for at in places], axis=0)
        rest = here[3 * quarter :]
        rest = jnp.concatenate([rest[:, i * THIRD : (i + 1) * THIRD] for i in range(3)], axis=0)
        outs[e][...] = jnp.concatenate([here[: 3 * quarter], rest], axis=1).astype(BF16)


def attend(slide_tiles, packs, heads, sets, count, exchange):
    queries, key_value = unpack(packs)
    rows = queries.shape[0]
    others = exchange(key_value)
    spread_of = len(others) + 1

    def layout(slide_tiles):
        return Layout(slide_tiles, heads, spread_of, sets, count)

    small = pl.BlockSpec(memory_space=pltpu.SMEM)
    whole = pl.BlockSpec(memory_space=pltpu.VMEM)
    params = pltpu.CompilerParams(vmem_limit_bytes=40 << 20)
    cost = pl.CostEstimate(
        flops=4 * rows * rows * LANES, bytes_accessed=6 * rows * LANES, transcendentals=rows * rows
    )
    partial = pl.pallas_call(
        functools.partial(attend_own_kernel, layout),
        in_specs=[small] + [whole] * 2,
        out_specs=whole,
        out_shape=jax.ShapeDtypeStruct((rows, LANES), F32),
        compiler_params=params,
        cost_estimate=cost,
        name="attend_own",
    )(slide_tiles, queries, key_value)
    packed = (rows // heads * 3 // 4, LANES)
    return pl.pallas_call(
        functools.partial(attend_others_kernel, layout, len(others)),
        in_specs=[small] + [whole] * (1 + spread_of),
        out_specs=[whole] * heads,
        out_shape=[jax.ShapeDtypeStruct(packed, BF16)] * heads,
        compiler_params=params,
        name="attend_others",
    )(slide_tiles, queries, partial, *others)


def partial_out_kernel(heads, tiles_of, spread_of, *refs):
    parts, w_out, outs = refs[:heads], refs[heads], refs[heads + 1 : heads + 1 + tiles_of]
    sorted_heads = refs[-1]
    a = lax.axis_index("blk") // spread_of
    quarter = parts[0].shape[0] // 3
    for e in range(heads):
        packed = parts[e][...].astype(F32)
        tail = packed[:, HD:]
        rest = jnp.concatenate([tail[i * quarter : (i + 1) * quarter] for i in range(3)], axis=1)
        sorted_heads[a ^ e] = jnp.concatenate([packed[:, :HD], rest], axis=0)
    attended = jnp.concatenate([sorted_heads[h] for h in range(heads)], axis=1).astype(BF16)
    product = dot(attended, w_out[...])
    count = product.shape[0] // tiles_of
    for d in range(tiles_of):
        outs[d][...] = product[d * count : (d + 1) * count].astype(outs[d].dtype)


def partial_out(parts, w_out, tiles_of, spread_of):
    heads, width = len(parts), w_out.shape[1]
    length = parts[0].shape[0] * 4 // 3
    count = length // tiles_of
    whole = pl.BlockSpec(memory_space=pltpu.VMEM)
    return pl.pallas_call(
        functools.partial(partial_out_kernel, heads, tiles_of, spread_of),
        in_specs=[whole] * (heads + 1),
        out_specs=[whole] * tiles_of,
        out_shape=[jax.ShapeDtypeStruct((count, width), F32 if d == 0 else BF16) for d in range(tiles_of)],
        scratch_shapes=[pltpu.VMEM((heads, length, HD), F32)],
        compiler_params=pltpu.CompilerParams(vmem_limit_bytes=24 << 20),
        name="partial_out",
    )(*parts, w_out)


def finish_kernel(emb, *refs):
    total = emb[...].astype(F32)
    for ref in refs[:-1]:
        total = total + ref[...].astype(F32)
    refs[-1][...] = total.astype(BF16)


def finish(emb, sums):
    return pl.pallas_call(
        finish_kernel,
        out_shape=jax.ShapeDtypeStruct(emb.shape, BF16),
        compiler_params=pltpu.CompilerParams(vmem_limit_bytes=24 << 20),
        name="finish",
    )(emb, *sums)


def shards(tiles_of, blks, tiles, wr, ws, we, wm, wq, wk, wv, wo, slide_tiles):
    count = tiles.shape[0]
    flat = tiles.reshape(count * SIDE * SIDE, tiles.shape[3])
    mid = wr.shape[1]
    heads = wq.shape[1] // HD
    spread_of = blks // heads

    def along(x, axis, size, step):
        return lax.ppermute(x, axis, [(i, i ^ step) for i in range(size)])

    def over_heads(blocks):
        return [blocks[0]] + [along(blocks[e], "blk", blks, e * spread_of) for e in range(1, heads)]

    emb = encode(flat, wr, ws.reshape(3, 3 * mid, mid), we, wm)
    embs = [emb] + [along(emb, "tile", tiles_of, d) for d in range(1, tiles_of)]
    sets = [range(tiles_of // 2), range(tiles_of // 2, tiles_of)]
    packs = []
    for members in sets:
        blocks = [embs[d] for d in members]
        if packs:
            *blocks, _ = lax.optimization_barrier((*blocks, packs[1]))
        packs += over_heads(project(blocks, wq, wk, wv, heads, spread_of))
    attended = attend(
        slide_tiles, packs, heads, sets, count,
        lambda x: [along(x, "blk", blks, f) for f in range(1, spread_of)],
    )
    sums = partial_out(over_heads(attended), wo, tiles_of, spread_of)
    sums = [sums[0]] + [along(sums[d], "tile", tiles_of, d) for d in range(1, tiles_of)]
    return finish(emb, sums)


def solution(mesh):
    placed = (
        P(("blk", "tile"), None, None, None),
        P(),
        P(),
        P(),
        P(),
        P(None, "tile"),
        P(None, "tile"),
        P(None, "tile"),
        P("tile", None),
        P(),
    )
    return jax.shard_map(
        functools.partial(shards, mesh.shape["tile"], mesh.shape["blk"]),
        mesh=mesh,
        in_specs=placed,
        out_specs=P(("blk", "tile"), None),
        check_vma=False,
    )
```
